32 devices in a mesh: req: 8 (over z, x), tok: 4 (over y, core).
Axes of the slice: x: 2, y: 2, z: 4, core: 2. Of those that a mesh axis runs over, the one named last changes fastest.
Arguments:
- queries: bfloat16 [4096, 2048], P('req', 'tok'), may hold values from -6 to 6
- suffix_kv: bfloat16 [4096, 2048], P('req'), may hold values from -6 to 6
- prefix_cache: bfloat16 [4096, 2048], P('req'), may hold values from -24 to 24
- q_gain: float32 [256], replicated, may hold values from 0.1 to 1.9
- k_gain: float32 [256], replicated, may hold values from 0.1 to 1.9
- lengths: int32 [8, 3], P('req'), may hold values from 1 to 256, 512 in all within a row
- group_of: int32 [8], replicated, may hold values from 0 to 1
- owner_order: int32 [8], replicated, may hold values from 0 to 7, each once
- residual: bfloat16 [4096, 2560], P('req'), may hold values from -6 to 6
- w_out: bfloat16 [2048, 2560], P('tok'), may hold values from -0.125 to 0.125
- attn_gain: float32 [2560], replicated, may hold values from 0.1 to 1.9
- ffn_in_gain: float32 [2560], replicated, may hold values from 0.1 to 1.9
- ffn_out_gain: float32 [2560], replicated, may hold values from 0.1 to 1.9
- w_gate: bfloat16 [2560, 10240], P(None, 'tok'), may hold values from -0.125 to 0.125
- w_up: bfloat16 [2560, 10240], P(None, 'tok'), may hold values from -0.125 to 0.125
- w_down: bfloat16 [10240, 2560], P('tok'), may hold values from -0.0625 to 0.0625
Outputs:
- layer_out: bfloat16 [4096, 2560], P(('req', 'tok'))
The draws below stay inside these ranges and needn't reach their ends.
Inputs may be any that keep to these rules, and one draw needn't show every extreme that they name: The 3 lengths of each req index sum to 512; the largest is exactly 256. `owner_order`: each req index appears once; entries g * 4 to g * 4 + 3 name the holders of group g's prefix.
All inputs are finite; a program needn't handle non-finite values.
Results may differ from the reference program's by a relative error of at most 0.02.
Values may be sent and summed in bfloat16 or wider, within the bound.
No kernel may reach another device: no remote copies, remote signals or barrier semaphores. Data moves between devices by JAX's collectives and lax.ppermute only.
A program may use at most 128 MiB of HBM per device.

```python
import math
import jax
import jax.numpy as jnp
import numpy as np
from jax import lax

D = 2560
H = 8
KVH = 4
HD = 256
FF = 10240
SUF_CAP = 512
PROWS = 512
REQ_DEV = 3
GROUPS = 2
SUF_MAX = 256
SUFFIX = 4096
CACHE_ROWS = 4096
N_REQ = 8


def draw_queries(key, part):
    own_key = jax.random.fold_in(key, 11)
    values_out = jnp.clip(jax.random.normal(own_key, (SUFFIX, H * HD), jnp.float32), -6.0, 6.0)
    return values_out.astype(jnp.bfloat16)


def draw_prefix_cache(key, part):
    own_key = jax.random.fold_in(key, 12)
    values_out = jnp.clip(jax.random.normal(own_key, (CACHE_ROWS, 2 * KVH * HD), jnp.float32), -6.0, 6.0)
    return values_out.astype(jnp.bfloat16)


def plant(entries, key, least, largest):
    extent = entries.shape
    index_at = [jax.random.randint(jax.random.fold_in(key, axis), (), 0, extent[axis]) for axis in range(len(extent))]
    entries = entries.at[tuple(index_at)].set(least)
    longest = extent.index(max(extent))
    index_at[longest] = (index_at[longest] + 1) % extent[longest]
    return entries.at[tuple(index_at)].set(largest)


def block_levels(key, shape, pieces, low, high):
    factor_of = 1.0
    for axis_at, shards_of in pieces:
        heights = jax.random.uniform(jax.random.fold_in(jax.random.fold_in(key, 6), axis_at), (shards_of,), jnp.float32, low / len(pieces), high / len(pieces))
        factor_of = factor_of * jnp.repeat(jnp.exp(heights), shape[axis_at] // shards_of).reshape((-1,) + (1,) * (len(shape) - 1 - axis_at))
    return factor_of


def profile(count, total, limit, slope):
    loads = [(1 << 20) // math.isqrt(grade ** slope) + 1 for grade in range(2, count + 1)]
    spare, given = total - limit - (count - 1), [1] * (count - 1)
    while spare > 0:
        movable = [i for i in range(count - 1) if given[i] < limit]
        mass, budget = sum([loads[i] for i in movable]), spare
        for i in movable:
            extra = min(limit - given[i], max(1, budget * loads[i] // mass), spare)
            given[i] = given[i] + extra
            spare = spare - extra
    return np.array([limit] + given)


def uneven(key, amount, total, bound, slope):
    if amount == 2:
        one = jax.random.randint(key, (), max(1, total - bound), min(bound, total - 1) + 1)
        return jnp.stack([one, total - one])
    tallies = jnp.asarray(profile(amount, total, bound, slope), jnp.int32)
    couples = (amount - 1) // 2
    donor, sink = tallies[1:1 + 2 * couples:2], tallies[2:2 + 2 * couples:2]
    margin = jnp.minimum(donor - 1, bound - sink)
    shifted = jax.random.randint(jax.random.fold_in(key, 1), (couples,), 0, 1 << 20) % (margin + 1)
    tallies = tallies.at[1:1 + 2 * couples:2].set(donor - shifted).at[2:2 + 2 * couples:2].set(sink + shifted)
    return tallies[jax.random.permutation(jax.random.fold_in(key, 2), amount)]


def gaussian(rng, dims, spread, limit, pieces=(), kind=jnp.bfloat16):
    drawn = jax.random.normal(rng, dims, jnp.float32) * spread
    if len(pieces) > 0:
        drawn = block_levels(rng, dims, pieces, -0.22, 0.18) * drawn
    return jnp.clip(drawn, min=-limit, max=limit).astype(kind)


def setup_inputs(seed: int = 0) -> dict:
    keys = jax.random.split(jax.random.key(seed), 17)
    return {
        "queries": draw_queries(jax.random.fold_in(keys[16], 71), 0),
        "suffix_kv": gaussian(keys[1], (SUFFIX, 2 * KVH * HD), 1.0, 6.0, ((0, 8),)),
        "prefix_cache": draw_prefix_cache(jax.random.fold_in(keys[16], 71), 0),
        "q_gain": jnp.clip(1.0 + 0.18 * jax.random.normal(keys[3], (HD,), jnp.float32), 0.1, 1.9),
        "k_gain": jnp.clip(1.0 + 0.18 * jax.random.normal(keys[4], (HD,), jnp.float32), 0.1, 1.9),
        "lengths": jax.vmap(lambda own: uneven(own, REQ_DEV, SUF_CAP, SUF_MAX, 2))(jax.random.split(keys[5], N_REQ)).reshape((N_REQ, REQ_DEV)).astype(jnp.int32),
        "group_of": plant(jax.random.randint(keys[6], (N_REQ,), 0, GROUPS), jax.random.fold_in(keys[6], 1), 0, GROUPS - 1).astype(jnp.int32),
        "owner_order": jax.random.permutation(keys[7], N_REQ).astype(jnp.int32),
        "residual": gaussian(keys[8], (SUFFIX, D), 1.0, 6.0, ((0, 8),)),
        "w_out": gaussian(keys[9], (H * HD, D), (H * HD) ** -0.5, 0.125, ((0, 4),)),
        "attn_gain": jnp.clip(1.0 + 0.18 * jax.random.normal(keys[10], (D,), jnp.float32), 0.1, 1.9),
        "ffn_in_gain": jnp.clip(1.0 + 0.18 * jax.random.normal(keys[11], (D,), jnp.float32), 0.1, 1.9),
        "ffn_out_gain": jnp.clip(1.0 + 0.18 * jax.random.normal(keys[12], (D,), jnp.float32), 0.1, 1.9),
        "w_gate": gaussian(keys[13], (D, FF), D ** -0.5, 0.125, ((1, 4),)),
        "w_up": gaussian(keys[14], (D, FF), D ** -0.5, 0.125, ((1, 4),)),
        "w_down": gaussian(keys[15], (FF, D), FF ** -0.5, 0.0625, ((0, 4),)),
    }


EPSILON = 1e-06
MASKED = -1e+30

def rms_scale(values_in, gain_vec):
    return values_in * lax.rsqrt(lax.optimization_barrier(jnp.mean(values_in * values_in, axis=-1, keepdims=True)) + EPSILON) * gain_vec

def reference(queries, suffix_kv, prefix_cache, q_gain, k_gain, lengths, group_of, owner_order, residual, w_out, attn_gain, ffn_in_gain, ffn_out_gain, w_gate, w_up, w_down):
    kv_width = KVH * HD
    head_ratio = H // KVH
    score_scale = HD ** (-0.5)
    owner_table = owner_order.reshape(GROUPS, N_REQ // GROUPS)
    cache_blocks = prefix_cache.reshape(N_REQ, PROWS, 2 * kv_width)
    query_blocks = queries.reshape(N_REQ, SUF_CAP, H, HD)
    suffix_blocks = suffix_kv.reshape(N_REQ, SUF_CAP, 2 * kv_width)
    positions = jnp.arange(SUF_CAP, dtype=jnp.int32)

    def one_index(req_index):
        query_normed = rms_scale(query_blocks[req_index].astype(jnp.float32), q_gain).astype(jnp.bfloat16)
        own_kv = suffix_blocks[req_index]
        suf_keys = rms_scale(own_kv[:, :kv_width].reshape(SUF_CAP, KVH, HD).astype(jnp.float32), k_gain).astype(jnp.bfloat16)
        suf_vals = own_kv[:, kv_width:].reshape(SUF_CAP, KVH, HD)
        owner_ids = jnp.take(owner_table, group_of[req_index], axis=0)
        shared = jnp.take(cache_blocks, owner_ids, axis=0).reshape(-1, 2 * kv_width)
        all_keys = jnp.concatenate([shared[:, :kv_width].reshape(-1, KVH, HD), suf_keys], axis=0)
        all_vals = jnp.concatenate([shared[:, kv_width:].reshape(-1, KVH, HD), suf_vals], axis=0)
        seg_ends = jnp.cumsum(lengths[req_index]).astype(jnp.int32)
        segment = lax.optimization_barrier(jnp.sum((positions[:, None] >= seg_ends[None, :]).astype(jnp.int32), axis=1))
        causal = (segment[:, None] == segment[None, :]) & (positions[None, :] <= positions[:, None])
        visible = jnp.concatenate([jnp.ones((SUF_CAP, shared.shape[0]), jnp.bool_), causal], axis=1)
        outputs = []
        for head_idx in range(H):
            kv_idx = head_idx // head_ratio
            scores = jnp.dot(query_normed[:, head_idx], all_keys[:, kv_idx].T, preferred_element_type=jnp.float32) * score_scale
            scores = jnp.where(visible, scores, MASKED)
            row_max = lax.optimization_barrier(jnp.max(scores, axis=-1, keepdims=True))
            weights = jnp.exp(scores - row_max)
            row_sum = lax.optimization_barrier(jnp.sum(weights, axis=-1, keepdims=True))
            head_out = jnp.dot(weights.astype(jnp.bfloat16), all_vals[:, kv_idx], preferred_element_type=jnp.float32) / row_sum
            outputs.append(head_out)
        return jnp.concatenate(outputs, axis=1).astype(jnp.bfloat16)
    attention = lax.map(one_index, jnp.arange(N_REQ, dtype=jnp.int32)).reshape(N_REQ * SUF_CAP, H * HD)
    projected = jnp.dot(attention, w_out, preferred_element_type=jnp.float32)
    mixed_rows = residual.astype(jnp.float32) + rms_scale(projected, attn_gain)
    normed = rms_scale(mixed_rows, ffn_in_gain).astype(jnp.bfloat16)
    gate = jnp.dot(normed, w_gate, preferred_element_type=jnp.float32)
    upward = jnp.dot(normed, w_up, preferred_element_type=jnp.float32)
    hidden = (jax.nn.gelu(gate, approximate=True) * upward).astype(jnp.bfloat16)
    down = jnp.dot(hidden, w_down, preferred_element_type=jnp.float32)
    return (mixed_rows + rms_scale(down, ffn_out_gain)).astype(jnp.bfloat16)
```

```python
import functools

import jax
import jax.numpy as jnp
from jax import lax
from jax.experimental import pallas as pl
from jax.experimental.pallas import tpu as pltpu
from jax.sharding import PartitionSpec as P

H = 8
KVH = 4
HD = 256
GROUPS = 2
EPSILON = 1e-06
MASKED = -1e30
CORES = 2
LINE = 4
BF16 = jnp.bfloat16
F32 = jnp.float32
ANY = pl.BlockSpec(memory_space=pl.ANY)
VMEM = pl.BlockSpec(memory_space=pltpu.VMEM)
SMEM = pl.BlockSpec(memory_space=pltpu.SMEM)


def mib(count):
    return count << 20


def rms(values_in):
    return values_in * lax.rsqrt(jnp.mean(values_in * values_in, axis=-1, keepdims=True) + EPSILON)


def norm_heads(values_in, gain_vec, head_count):
    row_count = values_in.shape[0]
    shaped = values_in.astype(F32).reshape(row_count, head_count, HD)
    return (rms(shaped) * gain_vec).astype(BF16).reshape(row_count, head_count * HD)


def attend(query_ref, state, head, rows, keys, values, visible):
    max_ref, sum_ref, acc_ref = state
    columns = slice(head * HD, (head + 1) * HD)
    scores = lax.dot_general(
        query_ref[rows, columns], keys, (((1,), (1,)), ((), ())), preferred_element_type=F32
    )
    block_max = jnp.max(scores if visible is None else jnp.where(visible, scores, MASKED), axis=1, keepdims=True)
    if visible is not None:
        scores = jnp.where(visible, scores, MASKED)
        weights = jnp.exp(scores - block_max)
        max_ref[head, rows, :] = jnp.broadcast_to(block_max, (scores.shape[0], 128))
        sum_ref[head, rows, :] = jnp.broadcast_to(
            jnp.sum(weights, axis=1, keepdims=True), (scores.shape[0], 128)
        )
        acc_ref[rows, columns] = jnp.dot(weights.astype(BF16), values, preferred_element_type=F32)
        return
    old_max = max_ref[head, rows, :]
    new_max = jnp.maximum(old_max, block_max)
    scale = jnp.exp(old_max - new_max)
    weights = jnp.exp(scores - new_max[:, :1])
    max_ref[head, rows, :] = new_max
    sum_ref[head, rows, :] = sum_ref[head, rows, :] * scale + jnp.sum(weights, axis=1, keepdims=True)
    acc_ref[rows, columns] = acc_ref[rows, columns] * scale[:, :1] + jnp.dot(
        weights.astype(BF16), values, preferred_element_type=F32
    )


def attention_kernel(block_count, heads, first, last, *refs):
    refs = list(refs)
    take = lambda count: [refs.pop(0) for _ in range(count)]
    (flags,) = take(1)
    if first:
        ends, query_ref, own_keys, own_values = take(4)
    else:
        query_ref, max_in, sum_in, acc_in = take(4)
    blocks = take(block_count)
    if last:
        (out_ref,) = take(1)
        held, sems, max_ref, sum_ref, acc_ref = refs
    else:
        max_ref, sum_ref, acc_ref = take(3)
        held, sems = refs
    state = (max_ref, sum_ref, acc_ref)
    for at, block in enumerate(blocks):

        @pl.when(flags[at] > 0)
        def _():
            pltpu.make_async_copy(block, held.at[at], sems.at[at]).start()

    row_count = query_ref.shape[0]
    step = min(256, row_count)
    if first:
        for begin in range(0, row_count, step):
            rows = slice(begin, begin + step)
            row_at = lax.broadcasted_iota(jnp.int32, (step, row_count), 0) + begin
            key_at = lax.broadcasted_iota(jnp.int32, (step, row_count), 1)
            visible = key_at <= row_at
            for which in range(ends.shape[0] - 1):
                visible &= (row_at >= ends[which]) == (key_at >= ends[which])
            for head in range(heads):
                attend(query_ref, state, head, rows, own_keys[...], own_values[...], visible)
    else:
        max_ref[...] = max_in[...]
        sum_ref[...] = sum_in[...]
        acc_ref[...] = acc_in[...]

    for at in range(block_count):

        @pl.when(flags[at] > 0)
        def _():
            pltpu.make_async_copy(blocks[at], held.at[at], sems.at[at]).wait()
            for begin in range(0, row_count, step):
                for head in range(heads):
                    attend(
                        query_ref,
                        state,
                        head,
                        slice(begin, begin + step),
                        held[at, :, :HD],
                        held[at, :, HD:],
                        None,
                    )

    if last:
        for head in range(heads):
            columns = slice(head * HD, (head + 1) * HD)
            out_ref[:, columns] = (acc_ref[:, columns] / sum_ref[head, :, :1]).astype(BF16)


def attention_call(flags, query, blocks, opening, state, last):
    row_count = query.shape[0]
    heads = query.shape[1] // HD
    shapes = [
        ((heads, row_count, 128), F32),
        ((heads, row_count, 128), F32),
        ((row_count, heads * HD), F32),
    ]
    first = state is None
    kernel = functools.partial(attention_kernel, len(blocks), heads, first, last)
    if first:
        operands = (flags, opening[0], query, opening[1], opening[2], *blocks)
        in_specs = [SMEM, SMEM] + [VMEM] * 3 + [ANY] * len(blocks)
    else:
        operands = (flags, query, *state, *blocks)
        in_specs = [SMEM] + [VMEM] * 4 + [ANY] * len(blocks)
    scratch = [
        pltpu.VMEM((len(blocks),) + blocks[0].shape, BF16),
        pltpu.SemaphoreType.DMA((len(blocks),)),
    ]
    if last:
        out_shape = jax.ShapeDtypeStruct(query.shape, BF16)
        out_specs = VMEM
        scratch += [pltpu.VMEM(shape, dtype) for shape, dtype in shapes]
    else:
        out_shape = [jax.ShapeDtypeStruct(shape, dtype) for shape, dtype in shapes]
        out_specs = [VMEM] * 3
    return pl.pallas_call(
        kernel,
        in_specs=in_specs,
        out_specs=out_specs,
        out_shape=out_shape,
        scratch_shapes=scratch,
        compiler_params=pltpu.CompilerParams(vmem_limit_bytes=mib(16)),
        cost_estimate=pl.CostEstimate(
            flops=8 * row_count * row_count * heads * HD,
            bytes_accessed=mib(4),
            transcendentals=2 * row_count * row_count * heads,
        ),
        name="attend_blocks",
    )(*operands)


def hold_kernel(gate_ref, up_ref, down_ref, _, gate_out, up_out, down_out, sems):
    copies = [
        pltpu.make_async_copy(source, target, sems.at[at])
        for at, (source, target) in enumerate(
            ((gate_ref, gate_out), (up_ref, up_out), (down_ref, down_out))
        )
    ]
    for copy in copies:
        copy.start()
    for copy in copies:
        copy.wait()


def hold_weights(gate, up, down, after):
    return pl.pallas_call(
        hold_kernel,
        in_specs=[ANY] * 4,
        out_specs=[VMEM] * 3,
        out_shape=[pltpu.VMEM(weight.shape, weight.dtype) for weight in (gate, up, down)],
        scratch_shapes=[pltpu.SemaphoreType.DMA((3,))],
        compiler_params=pltpu.CompilerParams(vmem_limit_bytes=mib(1)),
        cost_estimate=pl.CostEstimate(flops=0, bytes_accessed=2 * 3 * gate.size * 2, transcendentals=0),
        name="hold_weights",
    )(gate, up, down, after)


def project_kernel(pieces, *refs):
    begins = refs[0]
    heads_refs = refs[1 : 1 + pieces]
    weight_refs = refs[1 + pieces : 1 + 2 * pieces]
    residual_ref, gain_ref, in_gain_ref, mixed_ref, normed_ref = refs[1 + 2 * pieces : 6 + 2 * pieces]
    heads_held, weights_held, residual_held, sems = refs[6 + 2 * pieces :]
    share = mixed_ref.shape[0]
    weight_copies = [
        pltpu.make_async_copy(weight_refs[at], weights_held.at[at], sems.at[at])
        for at in range(pieces)
    ]
    row_copies = []
    for tile in range(CORES):
        begin = pl.multiple_of(begins[tile], share)
        row_copies.append(
            pltpu.make_async_copy(
                residual_ref.at[pl.ds(begin, share)],
                residual_held.at[pl.ds(tile * share, share)],
                sems.at[pieces + tile],
            )
        )
        for at in range(pieces):
            row_copies.append(
                pltpu.make_async_copy(
                    heads_refs[at].at[pl.ds(begin, share)],
                    heads_held.at[at, pl.ds(tile * share, share)],
                    sems.at[pieces + CORES + tile * pieces + at],
                )
            )
    for copy in row_copies + weight_copies:
        copy.start()
    for copy in row_copies:
        copy.wait()
    total = None
    for at in range(pieces):
        weight_copies[at].wait()
        product = jnp.dot(heads_held[at], weights_held[at], preferred_element_type=F32)
        total = product if total is None else total + product
    mixed = residual_held[...].astype(F32) + rms(total) * gain_ref[...]
    normed_ref[...] = (rms(mixed) * in_gain_ref[...]).astype(BF16)
    mixed_ref[...] = mixed[:share]


def project_rows(begins, heads_parts, weight_parts, residual, attn_gain, ffn_in_gain, share):
    pieces = len(heads_parts)
    width = residual.shape[1]
    rows = CORES * share
    depth = heads_parts[0].shape[1]
    return pl.pallas_call(
        functools.partial(project_kernel, pieces),
        in_specs=[SMEM] + [ANY] * (2 * pieces + 1) + [VMEM] * 2,
        out_specs=[VMEM] * 2,
        out_shape=[
            jax.ShapeDtypeStruct((share, width), F32),
            jax.ShapeDtypeStruct((rows, width), BF16),
        ],
        scratch_shapes=[
            pltpu.VMEM((pieces, rows, depth), BF16),
            pltpu.VMEM((pieces, depth, width), BF16),
            pltpu.VMEM((rows, width), BF16),
            pltpu.SemaphoreType.DMA((pieces + CORES + CORES * pieces,)),
        ],
        compiler_params=pltpu.CompilerParams(vmem_limit_bytes=mib(20)),
        cost_estimate=pl.CostEstimate(
            flops=2 * rows * pieces * depth * width, bytes_accessed=mib(14), transcendentals=0
        ),
        name="project_rows",
    )(begins, *heads_parts, *weight_parts, residual, attn_gain, ffn_in_gain)


def feed_kernel(rows_ref, gate_ref, up_ref, down_ref, keep_ref, send_ref, hidden_ref):
    share = keep_ref.shape[0]
    step = 256
    for begin in range(0, gate_ref.shape[1], step):
        columns = slice(begin, begin + step)
        gate = jnp.dot(rows_ref[...], gate_ref[:, columns], preferred_element_type=F32)
        upward = jnp.dot(rows_ref[...], up_ref[:, columns], preferred_element_type=F32)
        hidden_ref[:, columns] = (jax.nn.gelu(gate, approximate=True) * upward).astype(BF16)
    for begin in range(0, down_ref.shape[1], step):
        columns = slice(begin, begin + step)
        down = jnp.dot(hidden_ref[...], down_ref[:, columns], preferred_element_type=F32)
        keep_ref[:, columns] = down[:share]
        send_ref[:, columns] = down[share:].astype(BF16)


def feed_rows(rows, gate, up, down, share):
    count, width = rows.shape
    held = [pltpu.with_memory_space_constraint(weight, pltpu.VMEM) for weight in (gate, up, down)]
    return pl.pallas_call(
        feed_kernel,
        in_specs=[VMEM] * 4,
        out_specs=[VMEM] * 2,
        out_shape=[
            jax.ShapeDtypeStruct((share, width), F32),
            jax.ShapeDtypeStruct((count - share, width), BF16),
        ],
        scratch_shapes=[pltpu.VMEM((count, gate.shape[1]), BF16)],
        compiler_params=pltpu.CompilerParams(vmem_limit_bytes=mib(12)),
        cost_estimate=pl.CostEstimate(
            flops=6 * count * width * gate.shape[1],
            bytes_accessed=mib(4),
            transcendentals=count * gate.shape[1],
        ),
        name="feed_rows",
    )(rows, *held)


def join_kernel(keep_ref, other_ref, out_ref):
    out_ref[...] = (keep_ref[...] + other_ref[...].astype(F32)).astype(BF16)


def join(keep, other):
    return pl.pallas_call(
        join_kernel,
        out_shape=jax.ShapeDtypeStruct(keep.shape, BF16),
        compiler_params=pltpu.CompilerParams(vmem_limit_bytes=mib(8)),
        name="join",
    )(keep, other)


def finish_kernel(count, *refs):
    mixed_ref, keep_ref = refs[:2]
    gain_ref, out_ref = refs[2 + count :]
    total = keep_ref[...]
    for other in refs[2 : 2 + count]:
        total = total + other[...].astype(F32)
    out_ref[...] = (mixed_ref[...] + rms(total) * gain_ref[...]).astype(BF16)


def finish(mixed, keep, others, gain):
    return pl.pallas_call(
        functools.partial(finish_kernel, len(others)),
        out_shape=jax.ShapeDtypeStruct(mixed.shape, BF16),
        compiler_params=pltpu.CompilerParams(vmem_limit_bytes=mib(12)),
        name="finish",
    )(mixed, keep, *others, gain)


def local(
    queries,
    suffix_kv,
    prefix_cache,
    q_gain,
    k_gain,
    lengths,
    group_of,
    owner_order,
    residual,
    w_out,
    attn_gain,
    ffn_in_gain,
    ffn_out_gain,
    w_gate,
    w_up,
    w_down,
):
    req_count = lax.axis_size("req")
    tok_count = lax.axis_size("tok")
    req_index = lax.axis_index("req")
    tok_index = lax.axis_index("tok")
    across = req_count // LINE
    planes = tok_count // CORES
    row_count = queries.shape[0]
    share = row_count // tok_count
    heads_here = queries.shape[1] // HD
    head_ratio = H // KVH
    kv_first = tok_index * heads_here // head_ratio
    kv_width = KVH * HD

    def head_columns(rows_in, which):
        return lax.dynamic_slice_in_dim(rows_in, which * kv_width + kv_first * HD, HD, 1)

    def along(values_in, hops, reach):
        pairs = []
        for place in range(LINE):
            source_line = place - (reach - 1 if hops > 0 else 1 - reach)
            if 0 <= place + hops < LINE and 0 <= source_line < LINE:
                pairs += [
                    (place * across + col, (place + hops) * across + col) for col in range(across)
                ]
        return lax.ppermute(values_in, "req", pairs)

    def aside(values_in, shift, lines):
        pairs = [
            (place * across + col, place * across + (col + shift) % across)
            for place in lines
            for col in range(across)
        ]
        return lax.ppermute(values_in, "req", pairs)

    def other_core(values_in):
        return lax.ppermute(values_in, "tok", [(at, at ^ 1) for at in range(tok_count)])

    def plane_shift(values_in, shift):
        return lax.ppermute(
            values_in, "tok", [(at, (at + CORES * shift) % tok_count) for at in range(tok_count)]
        )

    own_block = jnp.concatenate([head_columns(prefix_cache, 0), head_columns(prefix_cache, 1)], axis=1)
    line_at, col_at = req_index // across, req_index % across
    lefts, rights = [own_block], [own_block]
    for reach in range(1, LINE):
        lefts.append(along(lefts[-1], 1, reach))
        rights.append(along(rights[-1], -1, reach))
    waves = [[] for _ in range(LINE + 1)]
    waves[0].append((own_block, line_at, 0))
    for shift in range(1, across):
        waves[1].append((aside(own_block, shift, range(LINE)), line_at, shift))
    for reach in range(1, LINE):
        waves[reach].append((lefts[reach], line_at - reach, 0))
        waves[reach].append((rights[reach], line_at + reach, 0))
        for shift in range(1, across):
            waves[reach + 1].append(
                (aside(lefts[reach], shift, range(reach, LINE)), line_at - reach, shift)
            )
            waves[reach + 1].append(
                (aside(rights[reach], shift, range(LINE - reach)), line_at + reach, shift)
            )

    weight_parts = []
    for shift in range(planes):
        part = w_out if shift == 0 else plane_shift(w_out, shift)
        weight_parts += [part, other_core(part)]

    query = norm_heads(queries, q_gain, heads_here) * jnp.asarray(HD ** (-0.5), BF16)
    own_keys = norm_heads(head_columns(suffix_kv, 0), k_gain, 1)
    own_values = head_columns(suffix_kv, 1)
    seg_ends = jnp.cumsum(lengths[0]).astype(jnp.int32)

    slots = jnp.arange(req_count, dtype=jnp.int32)
    place_of = jnp.sum((owner_order[None, :] == slots[:, None]) * slots[None, :], axis=1)
    member = (place_of // (req_count // GROUPS)) == group_of[req_index]

    def wanted(wave):
        lines = jnp.stack([jnp.asarray(line, jnp.int32) for _, line, _ in wave])
        shifts = jnp.asarray([shift for _, _, shift in wave], jnp.int32)
        sources = lines * across + (col_at - shifts) % across
        inside = (lines >= 0) & (lines < LINE)
        hit = (sources[:, None] == slots[None, :]) & member[None, :]
        return (inside & jnp.any(hit, axis=1)).astype(jnp.int32)

    calls = [waves[0] + waves[1], waves[2], waves[3], waves[4]]
    state = attention_call(
        wanted(calls[0]),
        query,
        [block for block, _, _ in calls[0]],
        (seg_ends, own_keys, own_values),
        None,
        False,
    )
    held = hold_weights(w_gate, w_up, w_down, state[0])
    for call in calls[1:]:
        state = attention_call(
            wanted(call), query, [block for block, _, _ in call], None, state, call is calls[-1]
        )
    attention = state

    heads_parts = []
    for shift in range(planes):
        part = attention if shift == 0 else plane_shift(attention, shift)
        heads_parts += [part, other_core(part)]

    plane_at, core_at = tok_index // CORES, tok_index % CORES

    def rows_of(shift):
        plane = (plane_at + shift) % planes
        begins = [(plane * CORES + core_at) * share, (plane * CORES + 1 - core_at) * share]
        return project_rows(
            jnp.stack(begins).astype(jnp.int32),
            heads_parts,
            weight_parts,
            residual,
            attn_gain[None],
            ffn_in_gain[None],
            share,
        )

    arrived = []
    for shift in range(planes - 1, 0, -1):
        _, normed = rows_of(shift)
        keep, send = feed_rows(normed, *held, share)
        arrived.append(plane_shift(join(keep, other_core(send)), shift))
    mixed, normed = rows_of(0)
    keep, send = feed_rows(normed, *held, share)
    return finish(mixed, keep, [other_core(send)] + arrived, ffn_out_gain[None])


def solution(mesh):
    in_specs = (
        P("req", "tok"),
        P("req", None),
        P("req", None),
        P(),
        P(),
        P("req", None),
        P(),
        P(),
        P("req", None),
        P("tok", None),
        P(),
        P(),
        P(),
        P(None, "tok"),
        P(None, "tok"),
        P("tok", None),
    )
    out_specs = P(("req", "tok"), None)
    return jax.shard_map(local, mesh=mesh, in_specs=in_specs, out_specs=out_specs, check_vma=False)
```

```python
import functools

import jax
import jax.numpy as jnp
from jax import lax
from jax.experimental import pallas as pl
from jax.experimental.pallas import tpu as pltpu
from jax.sharding import PartitionSpec as P

H = 8
KVH = 4
HD = 256
GROUPS = 2
EPSILON = 1e-06
MASKED = -1e30
CORES = 2
LINE = 4
BF16 = jnp.bfloat16
F32 = jnp.float32
ANY = pl.BlockSpec(memory_space=pl.ANY)
VMEM = pl.BlockSpec(memory_space=pltpu.VMEM)
SMEM = pl.BlockSpec(memory_space=pltpu.SMEM)
HBM = pl.BlockSpec(memory_space=pltpu.HBM)


def mib(count):
    return count << 20


def in_hbm(values_in):
    return pltpu.with_memory_space_constraint(values_in, pltpu.HBM)


def rms(values_in):
    return values_in * lax.rsqrt(jnp.mean(values_in * values_in, axis=-1, keepdims=True) + EPSILON)


def attend(query_ref, state, head, rows, keys, values, visible):
    max_ref, sum_ref, acc_ref = state
    columns = slice(head * HD, (head + 1) * HD)
    scores = lax.dot_general(
        query_ref[rows, columns], keys, (((1,), (1,)), ((), ())), preferred_element_type=F32
    )
    if visible is not None:
        scores = jnp.where(visible, scores, MASKED)
        block_max = jnp.max(scores, axis=1, keepdims=True)
        weights = jnp.exp(scores - block_max)
        max_ref[head, rows, :] = jnp.broadcast_to(block_max, (scores.shape[0], 128))
        sum_ref[head, rows, :] = jnp.broadcast_to(
            jnp.sum(weights, axis=1, keepdims=True), (scores.shape[0], 128)
        )
        acc_ref[rows, columns] = jnp.dot(weights.astype(BF16), values, preferred_element_type=F32)
        return
    old_max = max_ref[head, rows, :]
    new_max = jnp.maximum(old_max, jnp.max(scores, axis=1, keepdims=True))
    scale = jnp.exp(old_max - new_max)
    weights = jnp.exp(scores - new_max[:, :1])
    max_ref[head, rows, :] = new_max
    sum_ref[head, rows, :] = sum_ref[head, rows, :] * scale + jnp.sum(weights, axis=1, keepdims=True)
    acc_ref[rows, columns] = acc_ref[rows, columns] * scale[:, :1] + jnp.dot(
        weights.astype(BF16), values, preferred_element_type=F32
    )


def block_wanted(where, group_of, owner_order, block, across):
    line_hops, col_shift = block
    req_count = owner_order.shape[0]
    per_group = req_count // GROUPS
    req_index = where[0]
    line = req_index // across + line_hops
    source = line * across + lax.rem(lax.rem(req_index, across) + across - col_shift, across)
    holder = jnp.int32(-1)
    for slot in range(req_count):
        holder = jnp.where(owner_order[slot] == source, slot // per_group, holder)
    return (line >= 0) & (line < LINE) & (holder == group_of[req_index])


def attention_kernel(places, across, heads, first, parts, *refs):
    refs = list(refs)
    take = lambda count: [refs.pop(0) for _ in range(count)]
    where, group_of, owner_order = take(3)
    if first:
        lengths, queries, suffix, q_gain, k_gain = take(5)
    else:
        query_ref, max_in, sum_in, acc_in = take(4)
    blocks = take(len(places))
    if first:
        query_ref, max_ref, sum_ref, acc_ref, own_keys, own_values, held, sems, own_sems = refs
    elif parts:
        out_refs = take(parts)
        max_ref, sum_ref, acc_ref, held, sems = refs
    else:
        max_ref, sum_ref, acc_ref, held, sems = refs
    state = (max_ref, sum_ref, acc_ref)
    wanted = [block_wanted(where, group_of, owner_order, place, across) for place in places]
    for at, block in enumerate(blocks):

        @pl.when(wanted[at])
        def _():
            pltpu.make_async_copy(block, held.at[at], sems.at[at]).start()

    row_count = query_ref.shape[0]
    step = min(256, row_count)
    if first:
        begin = pl.multiple_of(where[2] * HD, HD)
        copies = [
            pltpu.make_async_copy(
                suffix.at[:, pl.ds(pl.multiple_of(begin + which * KVH * HD, HD), HD)],
                target,
                own_sems.at[which],
            )
            for which, target in enumerate((own_keys, own_values))
        ]
        for copy in copies:
            copy.start()
        for head in range(heads):
            columns = slice(head * HD, (head + 1) * HD)
            normed = (rms(queries[:, columns].astype(F32)) * q_gain[...]).astype(BF16)
            query_ref[:, columns] = normed * jnp.asarray(HD ** (-0.5), BF16)
        for copy in copies:
            copy.wait()
        own_keys[...] = (rms(own_keys[...].astype(F32)) * k_gain[...]).astype(BF16)
        ends = []
        for which in range(lengths.shape[1] - 1):
            ends.append(lengths[0, which] + (ends[-1] if ends else 0))
        for begin in range(0, row_count, step):
            rows = slice(begin, begin + step)
            seen = begin + step
            row_at = lax.broadcasted_iota(jnp.int32, (step, seen), 0) + begin
            key_at = lax.broadcasted_iota(jnp.int32, (step, seen), 1)
            visible = key_at <= row_at
            for end in ends:
                visible &= (row_at < end) | (key_at >= end)
            for head in range(heads):
                attend(query_ref, state, head, rows, own_keys[:seen, :], own_values[:seen, :], visible)
    else:
        max_ref[...] = max_in[...]
        sum_ref[...] = sum_in[...]
        acc_ref[...] = acc_in[...]

    for at in range(len(places)):

        @pl.when(wanted[at])
        def _():
            pltpu.make_async_copy(blocks[at], held.at[at], sems.at[at]).wait()
            for begin in range(0, row_count, step):
                for head in range(heads):
                    attend(
                        query_ref,
                        state,
                        head,
                        slice(begin, begin + step),
                        held[at, :, :HD],
                        held[at, :, HD:],
                        None,
                    )

    for at in range(parts):
        extent = row_count // parts
        begin = lax.rem(where[1] // CORES + at, parts) * extent
        rows = pl.ds(pl.multiple_of(begin, extent), extent)
        for head in range(heads):
            columns = slice(head * HD, (head + 1) * HD)
            out_refs[at][:, columns] = (acc_ref[rows, columns] / sum_ref[head, rows, :1]).astype(BF16)


def attention_call(scalars, across, opening, state, wave, parts):
    blocks = [block for block, _, _ in wave]
    places = [(hops, shift) for _, hops, shift in wave]
    query = opening[1] if state is None else state[0]
    row_count = query.shape[0]
    heads = query.shape[1] // HD
    shapes = [
        ((heads, row_count, 128), F32),
        ((heads, row_count, 128), F32),
        ((row_count, heads * HD), F32),
    ]
    first = state is None
    kernel = functools.partial(attention_kernel, places, across, heads, first, parts)
    if first:
        lengths, queries, suffix, q_gain, k_gain = opening
        operands = (*scalars, lengths, queries, in_hbm(suffix), q_gain, k_gain, *blocks)
        in_specs = [SMEM] * 4 + [VMEM, HBM, VMEM, VMEM] + [ANY] * len(blocks)
    else:
        operands = (*scalars, *state, *blocks)
        in_specs = [SMEM] * 3 + [VMEM] * 4 + [ANY] * len(blocks)
    scratch = [
        pltpu.VMEM((len(blocks),) + blocks[0].shape, BF16),
        pltpu.SemaphoreType.DMA((len(blocks),)),
    ]
    states = [jax.ShapeDtypeStruct(shape, dtype) for shape, dtype in shapes]
    if first:
        out_shape = [jax.ShapeDtypeStruct(query.shape, BF16)] + states
        scratch = (
            [pltpu.VMEM((row_count, HD), BF16)] * 2 + scratch + [pltpu.SemaphoreType.DMA((2,))]
        )
    elif parts:
        out_shape = [jax.ShapeDtypeStruct((row_count // parts, query.shape[1]), BF16)] * parts
        scratch = [pltpu.VMEM(shape, dtype) for shape, dtype in shapes] + scratch
    else:
        out_shape = states
    result = pl.pallas_call(
        kernel,
        in_specs=in_specs,
        out_specs=[VMEM] * len(out_shape),
        out_shape=out_shape,
        scratch_shapes=scratch,
        compiler_params=pltpu.CompilerParams(vmem_limit_bytes=mib(7)),
        cost_estimate=pl.CostEstimate(
            flops=8 * row_count * row_count * heads * HD,
            bytes_accessed=mib(4),
            transcendentals=2 * row_count * row_count * heads,
        ),
        name="attend_blocks",
    )(*operands)
    return result if first or parts else [query, *result]


def project_own_kernel(first_heads, second_heads, first_weight, second_weight, out_ref):
    total = jnp.dot(first_heads[...], first_weight[...], preferred_element_type=F32)
    total += jnp.dot(second_heads[...], second_weight[...], preferred_element_type=F32)
    out_ref[...] = total


def column_step(width):
    return 512 if width % 512 == 0 else 128


def project_own(heads_parts, weight_parts):
    rows, depth = heads_parts[0].shape
    width = weight_parts[0].shape[1]
    step = column_step(width)
    return pl.pallas_call(
        project_own_kernel,
        grid=(width // step,),
        in_specs=[pl.BlockSpec((rows, depth), lambda at: (0, 0))] * 2
        + [pl.BlockSpec((depth, step), lambda at: (0, at))] * 2,
        out_specs=pl.BlockSpec((rows, step), lambda at: (0, at)),
        out_shape=jax.ShapeDtypeStruct((rows, width), F32),
        compiler_params=pltpu.CompilerParams(vmem_limit_bytes=mib(7)),
        cost_estimate=pl.CostEstimate(
            flops=4 * rows * depth * width, bytes_accessed=mib(8), transcendentals=0
        ),
        name="project_own",
    )(*heads_parts, *weight_parts)


def project_kernel(pieces, group, *refs):
    where, residual_ref, own_ref = refs[:3]
    heads_refs = refs[3 : 3 + pieces]
    weight_refs = refs[3 + pieces : 3 + 2 * pieces]
    gain_ref, in_gain_ref, mixed_ref, normed_ref, total_ref, residual_held, sems = refs[3 + 2 * pieces :]
    share, width = mixed_ref.shape
    step = own_ref.shape[1]
    at = pl.program_id(0)
    planes = residual_ref.shape[0] // (CORES * share)
    core_at = lax.rem(where[1], CORES)
    first_row = lax.rem(where[1] // CORES + group, planes) * CORES * share
    copies = [
        pltpu.make_async_copy(
            residual_ref.at[pl.ds(pl.multiple_of(first_row + tile * share, share), share)],
            residual_held.at[pl.ds(tile * share, share)],
            sems.at[tile],
        )
        for tile in range(CORES)
    ]

    @pl.when(at == 0)
    def _():
        for copy in copies:
            copy.start()

    total = own_ref[...]
    for piece in range(pieces):
        total += jnp.dot(heads_refs[piece][...], weight_refs[piece][...], preferred_element_type=F32)
    total_ref[:, pl.ds(pl.multiple_of(at * step, step), step)] = total

    @pl.when(at == pl.num_programs(0) - 1)
    def _():
        for copy in copies:
            copy.wait()
        for tile in range(CORES):
            rows = slice(tile * share, (tile + 1) * share)
            mixed = residual_held[rows, :].astype(F32) + rms(total_ref[rows, :]) * gain_ref[...]
            target = jnp.where(core_at == tile, 0, share)
            normed_ref[pl.ds(pl.multiple_of(target, share), share), :] = (
                rms(mixed) * in_gain_ref[...]
            ).astype(BF16)

            @pl.when(core_at == tile)
            def _():
                mixed_ref[...] = mixed


def project_rows(where, group, residual, own_part, heads_parts, weight_parts, attn_gain, ffn_in_gain, share):
    pieces = len(heads_parts)
    rows, width = own_part.shape
    depth = heads_parts[0].shape[1]
    step = column_step(width)
    whole = lambda shape: pl.BlockSpec(shape, lambda at: (0, 0), pipeline_mode=pl.Buffered(1))
    return pl.pallas_call(
        functools.partial(project_kernel, pieces, group),
        grid=(width // step,),
        in_specs=[SMEM, HBM, pl.BlockSpec((rows, step), lambda at: (0, at))]
        + [whole((rows, depth))] * pieces
        + [pl.BlockSpec((depth, step), lambda at: (0, at))] * pieces
        + [whole((1, width))] * 2,
        out_specs=[whole((share, width)), whole((rows, width))],
        out_shape=[
            jax.ShapeDtypeStruct((share, width), F32),
            jax.ShapeDtypeStruct((rows, width), BF16),
        ],
        scratch_shapes=[
            pltpu.VMEM((rows, width), F32),
            pltpu.VMEM((rows, width), BF16),
            pltpu.SemaphoreType.DMA((CORES,)),
        ],
        compiler_params=pltpu.CompilerParams(vmem_limit_bytes=mib(11)),
        cost_estimate=pl.CostEstimate(
            flops=2 * rows * pieces * depth * width, bytes_accessed=mib(14), transcendentals=0
        ),
        name="project_rows",
    )(
        where,
        in_hbm(residual),
        own_part,
        *heads_parts,
        *weight_parts,
        attn_gain,
        ffn_in_gain,
    )


def feed_kernel(rows_ref, gate_ref, up_ref, down_ref, keep_ref, send_ref, hidden_ref):
    share = keep_ref.shape[0]
    step = 256
    for begin in range(0, gate_ref.shape[1], step):
        columns = slice(begin, begin + step)
        gate = jnp.dot(rows_ref[...], gate_ref[:, columns], preferred_element_type=F32)
        upward = jnp.dot(rows_ref[...], up_ref[:, columns], preferred_element_type=F32)
        hidden_ref[:, columns] = (jax.nn.gelu(gate, approximate=True) * upward).astype(BF16)
    for begin in range(0, down_ref.shape[1], step):
        columns = slice(begin, begin + step)
        down = jnp.dot(hidden_ref[...], down_ref[:, columns], preferred_element_type=F32)
        keep_ref[:, columns] = down[:share]
        send_ref[:, columns] = down[share:].astype(BF16)


def feed_rows(rows, gate, up, down, share):
    count, width = rows.shape
    held = [pltpu.with_memory_space_constraint(weight, pltpu.VMEM) for weight in (gate, up, down)]
    return pl.pallas_call(
        feed_kernel,
        in_specs=[VMEM] * 4,
        out_specs=[VMEM] * 2,
        out_shape=[
            jax.ShapeDtypeStruct((share, width), F32),
            jax.ShapeDtypeStruct((count - share, width), BF16),
        ],
        scratch_shapes=[pltpu.VMEM((count, gate.shape[1]), BF16)],
        compiler_params=pltpu.CompilerParams(vmem_limit_bytes=mib(7)),
        cost_estimate=pl.CostEstimate(
            flops=6 * count * width * gate.shape[1],
            bytes_accessed=mib(4),
            transcendentals=count * gate.shape[1],
        ),
        name="feed_rows",
    )(rows, *held)


def join_kernel(keep_ref, *refs):
    out_ref = refs[-1]
    half = keep_ref.shape[0] // 2
    for at in range(2):
        rows = slice(at * half, (at + 1) * half)
        out_ref[rows, :] = (keep_ref[rows, :] + refs[at][...].astype(F32)).astype(BF16)


def join(keep, other):
    return pl.pallas_call(
        join_kernel,
        out_shape=jax.ShapeDtypeStruct(keep.shape, BF16),
        compiler_params=pltpu.CompilerParams(vmem_limit_bytes=mib(8)),
        name="join",
    )(keep, *other)


def fold_kernel(keep_ref, *refs):
    total = keep_ref[...]
    for other in refs[:-1]:
        total = total + other[...].astype(F32)
    refs[-1][...] = total


def fold(keep, arrived):
    return pl.pallas_call(
        fold_kernel,
        out_shape=jax.ShapeDtypeStruct(keep.shape, F32),
        compiler_params=pltpu.CompilerParams(vmem_limit_bytes=mib(7)),
        name="fold",
    )(keep, *arrived)


def finish_kernel(mixed_ref, total_ref, *refs):
    gain_ref, out_ref = refs[-2:]
    half = total_ref.shape[0] // 2
    for at in range(2):
        rows = slice(at * half, (at + 1) * half)
        total = total_ref[rows, :] + refs[at][...].astype(F32)
        out_ref[rows, :] = (mixed_ref[rows, :] + rms(total) * gain_ref[...]).astype(BF16)


def finish(mixed, total, other, gain):
    return pl.pallas_call(
        finish_kernel,
        out_shape=jax.ShapeDtypeStruct(mixed.shape, BF16),
        compiler_params=pltpu.CompilerParams(vmem_limit_bytes=mib(7)),
        name="finish",
    )(mixed, total, *other, gain)


def local(
    queries,
    suffix_kv,
    prefix_cache,
    q_gain,
    k_gain,
    lengths,
    group_of,
    owner_order,
    residual,
    w_out,
    attn_gain,
    ffn_in_gain,
    ffn_out_gain,
    w_gate,
    w_up,
    w_down,
):
    req_count = lax.axis_size("req")
    tok_count = lax.axis_size("tok")
    req_index = lax.axis_index("req")
    tok_index = lax.axis_index("tok")
    across = req_count // LINE
    planes = tok_count // CORES
    row_count = queries.shape[0]
    share = row_count // tok_count
    heads_here = queries.shape[1] // HD
    head_ratio = H // KVH
    kv_first = tok_index * heads_here // head_ratio
    kv_width = KVH * HD

    def head_columns(rows_in, which):
        return lax.dynamic_slice_in_dim(rows_in, which * kv_width + kv_first * HD, HD, 1)

    def along(values_in, hops, reach):
        pairs = []
        for place in range(LINE):
            source_line = place - (reach - 1 if hops > 0 else 1 - reach)
            if 0 <= place + hops < LINE and 0 <= source_line < LINE:
                pairs += [
                    (place * across + col, (place + hops) * across + col) for col in range(across)
                ]
        return lax.ppermute(values_in, "req", pairs)

    def aside(values_in, shift, lines):
        pairs = [
            (place * across + col, place * across + (col + shift) % across)
            for place in lines
            for col in range(across)
        ]
        return lax.ppermute(values_in, "req", pairs)

    def other_core(values_in):
        return lax.ppermute(values_in, "tok", [(at, at ^ 1) for at in range(tok_count)])

    def plane_shift(values_in, shift):
        return lax.ppermute(
            values_in, "tok", [(at, (at + CORES * shift) % tok_count) for at in range(tok_count)]
        )

    own_block = jnp.concatenate([head_columns(prefix_cache, 0), head_columns(prefix_cache, 1)], axis=1)
    where = jnp.stack([req_index, tok_index, kv_first]).astype(jnp.int32)
    scalars = (where, group_of, owner_order)
    plane_weights = [w_out] + [plane_shift(w_out, shift) for shift in range(1, planes)]
    state = attention_call(
        scalars,
        across,
        (lengths, queries, suffix_kv, q_gain[None], k_gain[None]),
        None,
        [(own_block, 0, 0)],
        0,
    )
    earlier = state
    left = right = own_block
    wave = [(aside(own_block, shift, range(LINE)), 0, shift) for shift in range(1, across)]
    for reach in range(1, LINE):
        if reach > 1:
            left, right, _ = lax.optimization_barrier((left, right, earlier[1]))
            earlier = state
        left, right = along(left, 1, reach), along(right, -1, reach)
        later = []
        for block, hops, lines in (
            (left, -reach, range(reach, LINE)),
            (right, reach, range(LINE - reach)),
        ):
            wave.append((block, hops, 0))
            later += [(aside(block, shift, lines), hops, shift) for shift in range(1, across)]
        state = attention_call(scalars, across, None, state, wave, 0)
        wave = later
    attention = attention_call(scalars, across, None, state, wave, planes)

    plane_weights[1:], attention = lax.optimization_barrier((plane_weights[1:], attention))
    weight_parts = [[part, other_core(part)] for part in plane_weights]
    far_weights = [part for parts in weight_parts[1:] for part in parts]
    order = list(range(planes - 1, -1, -1))
    far_heads = {}
    previous = None
    for group in order:
        sent = [attention[(group + shift) % planes] for shift in range(1, planes)]
        if previous is not None:
            sent, previous = lax.optimization_barrier((sent, previous))
        previous = [plane_shift(part, shift) for shift, part in enumerate(sent, 1)]
        far_heads[group] = previous
    own_heads = [[attention[group], other_core(attention[group])] for group in range(planes)]

    def rows_of(group, own_part):
        heads_parts = []
        for part in far_heads[group]:
            heads_parts += [part, other_core(part)]
        return project_rows(
            where,
            group,
            residual,
            own_part,
            heads_parts,
            far_weights,
            attn_gain[None],
            ffn_in_gain[None],
            share,
        )

    def swap(values_in):
        half = values_in.shape[0] // 2
        return [other_core(values_in[:half]), other_core(values_in[half:])]

    own_part = project_own(own_heads[order[0]], weight_parts[0])
    far_heads[order[0]], own_part = lax.optimization_barrier((far_heads[order[0]], own_part))
    mixed, normed = rows_of(order[0], own_part)
    arrived = []
    for at, group in enumerate(order[:-1]):
        keep, send = feed_rows(normed, w_gate, w_up, w_down, share)
        later = order[at + 1]
        own_heads[later], send = lax.optimization_barrier((own_heads[later], send))
        other = swap(send)
        own_part = project_own(own_heads[later], weight_parts[0])
        other, own_part = lax.optimization_barrier((other, own_part))
        joined = join(keep, other)
        own_part, joined = lax.optimization_barrier((own_part, joined))
        arrived.append(plane_shift(joined, group))
        mixed, normed = rows_of(later, own_part)
    keep, send = feed_rows(normed, w_gate, w_up, w_down, share)
    send, arrived = lax.optimization_barrier((send, arrived))
    return finish(mixed, fold(keep, arrived), swap(send), ffn_out_gain[None])


def solution(mesh):
    in_specs = (
        P("req", "tok"),
        P("req", None),
        P("req", None),
        P(),
        P(),
        P("req", None),
        P(),
        P(),
        P("req", None),
        P("tok", None),
        P(),
        P(),
        P(),
        P(None, "tok"),
        P(None, "tok"),
        P("tok", None),
    )
    out_specs = P(("req", "tok"), None)
    return jax.shard_map(local, mesh=mesh, in_specs=in_specs, out_specs=out_specs, check_vma=False)
```

```python
import functools

import jax
import jax.numpy as jnp
from jax import lax
from jax.experimental import pallas as pl
from jax.experimental.pallas import tpu as pltpu
from jax.sharding import PartitionSpec as P

H = 8
KVH = 4
HD = 256
GROUPS = 2
EPSILON = 1e-06
MASKED = -1e30
CORES = 2
LINE = 4
NUMBERS = 3
FEED_LIMIT = 25
BF16 = jnp.bfloat16
F32 = jnp.float32
ANY = pl.BlockSpec(memory_space=pl.ANY)
VMEM = pl.BlockSpec(memory_space=pltpu.VMEM)
SMEM = pl.BlockSpec(memory_space=pltpu.SMEM)
HBM = pl.BlockSpec(memory_space=pltpu.HBM)


def mib(count):
    return count << 20


def in_vmem(values_in):
    return pltpu.with_memory_space_constraint(values_in, pltpu.VMEM)


def in_hbm(values_in):
    return pltpu.with_memory_space_constraint(values_in, pltpu.HBM)


def rms(values_in):
    return values_in * lax.rsqrt(jnp.mean(values_in * values_in, axis=-1, keepdims=True) + EPSILON)


def attend(query_ref, state, head, rows, keys, values, visible):
    max_ref, sum_ref, acc_ref = state
    columns = slice(head * HD, (head + 1) * HD)
    scores = lax.dot_general(
        query_ref[rows, columns], keys, (((1,), (1,)), ((), ())), preferred_element_type=F32
    )
    if visible is not None:
        scores = jnp.where(visible, scores, MASKED)
        block_max = jnp.max(scores, axis=1, keepdims=True)
        weights = jnp.exp(scores - block_max)
        max_ref[head, rows, :] = jnp.broadcast_to(block_max, (scores.shape[0], 128))
        sum_ref[head, rows, :] = jnp.broadcast_to(
            jnp.sum(weights, axis=1, keepdims=True), (scores.shape[0], 128)
        )
        acc_ref[rows, columns] = jnp.dot(weights.astype(BF16), values, preferred_element_type=F32)
        return
    old_max = max_ref[head, rows, :]
    new_max = jnp.maximum(old_max, jnp.max(scores, axis=1, keepdims=True))
    scale = jnp.exp(old_max - new_max)
    weights = jnp.exp(scores - new_max[:, :1])
    max_ref[head, rows, :] = new_max
    sum_ref[head, rows, :] = sum_ref[head, rows, :] * scale + jnp.sum(weights, axis=1, keepdims=True)
    acc_ref[rows, columns] = acc_ref[rows, columns] * scale[:, :1] + jnp.dot(
        weights.astype(BF16), values, preferred_element_type=F32
    )


def block_wanted(numbers, place, across, req_count):
    source_lines, col_shift = place
    per_group = req_count // GROUPS
    req_index = numbers[0]
    line = req_index // across
    source_line = jnp.int32(-1)
    for at, source in enumerate(source_lines):
        if source >= 0:
            source_line = jnp.where(line == at, source, source_line)
    source = source_line * across + lax.rem(lax.rem(req_index, across) + across - col_shift, across)
    holder = jnp.int32(-1)
    for slot in range(req_count):
        holder = jnp.where(numbers[NUMBERS + req_count + slot] == source, slot // per_group, holder)
    return (source_line >= 0) & (holder == numbers[NUMBERS + req_index])


def attention_kernel(places, counts, across, req_count, heads, first, parts, near, *refs):
    refs = list(refs)
    take = lambda count: [refs.pop(0) for _ in range(count)]
    (numbers,) = take(1)
    if first:
        queries_ref, suffix, gains = take(3)
    else:
        query_ref, max_in, sum_in, acc_in = take(4)
    blocks = [take(count) for count in counts]
    take(near)
    if first:
        query_ref, max_ref, sum_ref, acc_ref, queries, own_keys, own_values, held, sems, own_sems = refs
    elif parts:
        out_refs = take(parts)
        max_ref, sum_ref, acc_ref, held, sems = refs
    else:
        max_ref, sum_ref, acc_ref = take(3)
        held, sems = refs
    state = (max_ref, sum_ref, acc_ref)
    wanted = [block_wanted(numbers, place, across, req_count) for place in places]

    def copies_of(at):
        extent = held.shape[1] // counts[at]
        return [
            pltpu.make_async_copy(
                block, held.at[at, pl.ds(piece * extent, extent)], sems.at[at, piece]
            )
            for piece, block in enumerate(blocks[at])
        ]

    for at in range(len(places)):

        @pl.when(wanted[at])
        def _():
            for copy in copies_of(at):
                copy.start()

    row_count = query_ref.shape[0]
    step = min(256, row_count)
    if first:
        begin = pl.multiple_of(numbers[2] * HD, HD)
        copies = [pltpu.make_async_copy(queries_ref, queries, own_sems.at[2])] + [
            pltpu.make_async_copy(
                suffix.at[:, pl.ds(pl.multiple_of(begin + which * KVH * HD, HD), HD)],
                target,
                own_sems.at[which],
            )
            for which, target in enumerate((own_keys, own_values))
        ]
        for copy in copies:
            copy.start()
        copies[0].wait()
        for head in range(heads):
            columns = slice(head * HD, (head + 1) * HD)
            normed = (rms(queries[:, columns].astype(F32)) * gains[:1, :]).astype(BF16)
            query_ref[:, columns] = normed * jnp.asarray(HD ** (-0.5), BF16)
        for copy in copies[1:]:
            copy.wait()
        own_keys[...] = (rms(own_keys[...].astype(F32)) * gains[1:, :]).astype(BF16)
        ends = []
        first_length = NUMBERS + 2 * req_count
        for at in range(first_length, numbers.shape[0] - 1):
            ends.append(numbers[at] + (ends[-1] if ends else 0))
        for begin in range(0, row_count, step):
            rows = slice(begin, begin + step)
            seen = begin + step
            row_at = lax.broadcasted_iota(jnp.int32, (step, seen), 0) + begin
            key_at = lax.broadcasted_iota(jnp.int32, (step, seen), 1)
            visible = key_at <= row_at
            for end in ends:
                visible &= (row_at < end) | (key_at >= end)
            for head in range(heads):
                attend(query_ref, state, head, rows, own_keys[:seen, :], own_values[:seen, :], visible)
    else:
        max_ref[...] = max_in[...]
        sum_ref[...] = sum_in[...]
        acc_ref[...] = acc_in[...]

    for at in range(len(places)):

        @pl.when(wanted[at])
        def _():
            for copy in copies_of(at):
                copy.wait()

            @pl.loop(0, row_count // step)
            def _(turn):
                rows = pl.ds(pl.multiple_of(turn * step, step), step)
                for head in range(heads):
                    attend(query_ref, state, head, rows, held[at, :, :HD], held[at, :, HD:], None)


    for at in range(parts):
        extent = row_count // parts
        begin = lax.rem(numbers[1] // CORES + at, parts) * extent
        rows = pl.ds(pl.multiple_of(begin, extent), extent)
        for head in range(heads):
            columns = slice(head * HD, (head + 1) * HD)
            out_refs[at][:, columns] = (acc_ref[rows, columns] / sum_ref[head, rows, :1]).astype(BF16)


def attention_call(numbers, across, req_count, opening, state, wave, parts, near=()):
    blocks = [block for parts_of, _, _ in wave for block in parts_of]
    counts = [len(parts_of) for parts_of, _, _ in wave]
    places = [(sources, shift) for _, sources, shift in wave]
    query = opening[0] if state is None else state[0]
    row_count = query.shape[0]
    heads = query.shape[1] // HD
    shapes = [
        ((heads, row_count, 128), F32),
        ((heads, row_count, 128), F32),
        ((row_count, heads * HD), F32),
    ]
    first = state is None
    kernel = functools.partial(attention_kernel, places, counts, across, req_count, heads, first, parts, len(near))
    if first:
        queries, suffix, gains = opening
        operands = (numbers, in_hbm(queries), in_hbm(suffix), gains, *blocks)
        in_specs = [SMEM, HBM, HBM, VMEM] + [ANY] * len(blocks)
    else:
        operands = (numbers, *state, *blocks, *[in_vmem(part) for part in near])
        in_specs = [SMEM] + [VMEM] * 4 + [ANY] * len(blocks) + [VMEM] * len(near)
    scratch = [
        pltpu.VMEM((len(wave), row_count, 2 * HD), BF16),
        pltpu.SemaphoreType.DMA((len(wave), 2)),
    ]
    states = [jax.ShapeDtypeStruct(shape, dtype) for shape, dtype in shapes]
    if first:
        out_shape = [jax.ShapeDtypeStruct(query.shape, BF16)] + states
        scratch = (
            [pltpu.VMEM(query.shape, BF16)]
            + [pltpu.VMEM((row_count, HD), BF16)] * 2
            + scratch
            + [pltpu.SemaphoreType.DMA((3,))]
        )
    elif parts:
        out_shape = [jax.ShapeDtypeStruct((row_count // parts, query.shape[1]), BF16)] * parts
        scratch = [pltpu.VMEM(shape, dtype) for shape, dtype in shapes] + scratch
    else:
        out_shape = states
    result = pl.pallas_call(
        kernel,
        in_specs=in_specs,
        out_specs=[VMEM] * len(out_shape),
        out_shape=out_shape,
        scratch_shapes=scratch,
        compiler_params=pltpu.CompilerParams(vmem_limit_bytes=mib(7)),
        cost_estimate=pl.CostEstimate(
            flops=8 * row_count * row_count * heads * HD,
            bytes_accessed=mib(4),
            transcendentals=2 * row_count * row_count * heads,
        ),
        name="attend_blocks",
    )(*operands)
    return result if first or parts else [query, *result]


def pick_kernel(lines, numbers, upper_ref, lower_ref, out_ref):
    upper = numbers[0] >= lines

    @pl.when(upper)
    def _():
        out_ref[...] = upper_ref[...]

    @pl.when(jnp.logical_not(upper))
    def _():
        out_ref[...] = lower_ref[...]


def pick(numbers, across, upper, lower):
    return pl.pallas_call(
        functools.partial(pick_kernel, across * LINE // 2),
        in_specs=[SMEM, VMEM, VMEM],
        out_specs=VMEM,
        out_shape=jax.ShapeDtypeStruct(upper.shape, upper.dtype),
        compiler_params=pltpu.CompilerParams(vmem_limit_bytes=mib(4)),
        name="pick",
    )(numbers, upper, lower)


def column_step(width):
    return 512 if width % 512 == 0 else 128


def feed_kernel(pieces, group, planes, *refs):
    refs = list(refs)
    take = lambda count: [refs.pop(0) for _ in range(count)]
    (numbers,), heads_refs, (gains,) = take(1), take(pieces), take(1)
    (gate_ref, up_ref), weight_refs = take(2), take(pieces - 2)
    down_source, residual_ref, *near_sources = take(4)
    (keep_ref, *send_refs), mixed_refs = take(3), take(int(group == 0))
    spare, total_ref, normed_ref, down_ref, sems = refs
    share, width = keep_ref.shape
    hidden = gate_ref.shape[1]
    core_at = lax.rem(numbers[1], CORES)
    first_row = lax.rem(numbers[1] // CORES + group, planes) * CORES * share
    step, unroll = 512, 5

    def columns_of(at, extent):
        return pl.ds(at * extent if isinstance(at, int) else pl.multiple_of(at * extent, extent), extent)

    residual_copies = []
    for tile in range(CORES):
        target = pl.multiple_of(jnp.where(core_at == tile, 0, share), share)
        residual_copies.append(
            pltpu.make_async_copy(
                residual_ref.at[pl.ds(pl.multiple_of(first_row + tile * share, share), share)],
                spare.at[pl.ds(target, share), pl.ds(0, width)],
                sems.at[tile],
            )
        )
    depth = near_sources[0].shape[0]
    near_copies = [
        pltpu.make_async_copy(source, down_ref.at[pl.ds(at * depth, depth)], sems.at[CORES + at])
        for at, source in enumerate(near_sources)
    ]
    down_copies = [
        pltpu.make_async_copy(down_source.at[rows], down_ref.at[rows], sems.at[CORES + 2 + at])
        for at, rows in enumerate((pl.ds(0, 2 * depth), pl.ds(2 * depth, hidden - 2 * depth)))
    ]
    for copy in [*near_copies, *residual_copies, down_copies[1]]:
        copy.start()
    wide = column_step(width)

    @pl.loop(0, width // wide)
    def _(at):
        columns = columns_of(at, wide)
        total = jnp.dot(heads_refs[2][...], weight_refs[0][:, columns], preferred_element_type=F32)
        for piece in range(3, pieces):
            total += jnp.dot(
                heads_refs[piece][...], weight_refs[piece - 2][:, columns], preferred_element_type=F32
            )
        total_ref[:, columns] = total

    for copy in near_copies:
        copy.wait()

    @pl.loop(0, width // wide)
    def _(at):
        columns = columns_of(at, wide)
        total = total_ref[:, columns]
        for piece in range(2):
            total += jnp.dot(
                heads_refs[piece][...],
                down_ref[piece * depth : (piece + 1) * depth, columns],
                preferred_element_type=F32,
            )
        total_ref[:, columns] = total

    down_copies[0].start()
    for copy in residual_copies:
        copy.wait()
    extent = min(64, share)

    @pl.loop(0, CORES * share // extent)
    def _(at):
        rows = pl.ds(pl.multiple_of(at * extent, extent), extent)
        source = lax.rem(at * extent + core_at * share, CORES * share)
        total = total_ref[pl.ds(pl.multiple_of(source, extent), extent), :]
        mixed = spare[rows, :width].astype(F32) + rms(total) * gains[0:1, :]
        normed_ref[rows, :] = (rms(mixed) * gains[1:2, :]).astype(BF16)
        for mixed_ref in mixed_refs:

            @pl.when(at < share // extent)
            def _():
                mixed_ref[rows, :] = mixed

    @pl.loop(0, hidden // step, unroll=unroll)
    def _(at):
        columns = columns_of(at, step)
        gate = jnp.dot(normed_ref[...], gate_ref[:, columns], preferred_element_type=F32)
        upward = jnp.dot(normed_ref[...], up_ref[:, columns], preferred_element_type=F32)
        spare[:, columns] = (jax.nn.gelu(gate, approximate=True) * upward).astype(BF16)

    for copy in down_copies:
        copy.wait()

    @pl.loop(0, width // step, unroll=unroll)
    def _(at):
        columns = columns_of(at, step)
        down = jnp.dot(spare[:, :hidden], down_ref[:, columns], preferred_element_type=F32)
        keep_ref[:, columns] = down[:share]
        for at_send, send_ref in enumerate(send_refs):
            begin = share + at_send * send_ref.shape[0]
            send_ref[:, columns] = down[begin : begin + send_ref.shape[0]].astype(BF16)


def feed_rows(
    numbers, group, planes, residual, heads_parts, near_weights, far_weights, gains, feed_weights
):
    pieces = len(heads_parts)
    rows, depth = heads_parts[0].shape
    width = residual.shape[1]
    share = rows // CORES
    hidden = feed_weights[0].shape[1]
    return pl.pallas_call(
        functools.partial(feed_kernel, pieces, group, planes),
        in_specs=[SMEM] + [VMEM] * (2 * pieces + 1) + [HBM] * 4,
        out_specs=[VMEM] * (3 + (group == 0)),
        out_shape=[pltpu.VMEM((share, width), F32)]
        + [pltpu.VMEM((share // 2, width), BF16)] * 2
        + [pltpu.VMEM((share, width), F32)] * (group == 0),
        scratch_shapes=[
            pltpu.VMEM((rows, max(width, hidden)), BF16),
            pltpu.VMEM((rows, width), F32),
            pltpu.VMEM((rows, width), BF16),
            pltpu.VMEM((hidden, width), BF16),
            pltpu.SemaphoreType.DMA((CORES + 4,)),
        ],
        compiler_params=pltpu.CompilerParams(vmem_limit_bytes=mib(FEED_LIMIT)),
        cost_estimate=pl.CostEstimate(
            flops=2 * rows * width * (pieces * heads_parts[0].shape[1] + 3 * hidden),
            bytes_accessed=mib(16),
            transcendentals=rows * hidden,
        ),
        name="feed_rows",
    )(
        numbers,
        *heads_parts,
        gains,
        *[in_vmem(part) for part in (*feed_weights[:2], *far_weights)],
        *[in_hbm(part) for part in (feed_weights[2], residual, *near_weights)],
    )


def join_kernel(keep_ref, *refs):
    out_ref = refs[-1]
    half = keep_ref.shape[0] // 2
    for at in range(2):
        rows = slice(at * half, (at + 1) * half)
        out_ref[rows, :] = (keep_ref[rows, :] + refs[at][...].astype(F32)).astype(BF16)


def join(keep, other):
    return pl.pallas_call(
        join_kernel,
        out_shape=jax.ShapeDtypeStruct(keep.shape, BF16),
        compiler_params=pltpu.CompilerParams(vmem_limit_bytes=mib(8)),
        name="join",
    )(keep, *other)


def fold_kernel(keep_ref, *refs):
    total = keep_ref[...]
    for other in refs[:-1]:
        total = total + other[...].astype(F32)
    refs[-1][...] = total


def fold(keep, arrived):
    return pl.pallas_call(
        fold_kernel,
        out_shape=jax.ShapeDtypeStruct(keep.shape, F32),
        compiler_params=pltpu.CompilerParams(vmem_limit_bytes=mib(7)),
        name="fold",
    )(keep, *arrived)


def finish_kernel(mixed_ref, total_ref, *refs):
    gains_ref, out_ref = refs[-2:]
    half = total_ref.shape[0] // 2
    for at in range(2):
        rows = slice(at * half, (at + 1) * half)
        total = total_ref[rows, :] + refs[at][...].astype(F32)
        out_ref[rows, :] = (mixed_ref[rows, :] + rms(total) * gains_ref[2:3, :]).astype(BF16)


def finish(mixed, total, other, gains):
    return pl.pallas_call(
        finish_kernel,
        out_shape=jax.ShapeDtypeStruct(mixed.shape, BF16),
        compiler_params=pltpu.CompilerParams(vmem_limit_bytes=mib(7)),
        name="finish",
    )(mixed, total, *other, gains)


def local(
    queries,
    suffix_kv,
    prefix_cache,
    q_gain,
    k_gain,
    lengths,
    group_of,
    owner_order,
    residual,
    w_out,
    attn_gain,
    ffn_in_gain,
    ffn_out_gain,
    w_gate,
    w_up,
    w_down,
):
    req_count = lax.axis_size("req")
    tok_count = lax.axis_size("tok")
    req_index = lax.axis_index("req")
    tok_index = lax.axis_index("tok")
    across = req_count // LINE
    planes = tok_count // CORES
    row_count = queries.shape[0]
    share = row_count // tok_count
    heads_here = queries.shape[1] // HD
    head_ratio = H // KVH
    kv_first = tok_index * heads_here // head_ratio
    kv_width = KVH * HD

    def head_columns(rows_in, which):
        return lax.dynamic_slice_in_dim(rows_in, which * kv_width + kv_first * HD, HD, 1)

    def move(values_in, lines, shift=0):
        pairs = [
            (source * across + col, target * across + (col + shift) % across)
            for source, target in lines
            for col in range(across)
        ]
        return lax.ppermute(values_in, "req", pairs)

    def other_core(values_in):
        return lax.ppermute(values_in, "tok", [(at, at ^ 1) for at in range(tok_count)])

    def plane_shift(values_in, shift):
        return lax.ppermute(
            values_in, "tok", [(at, (at + CORES * shift) % tok_count) for at in range(tok_count)]
        )

    own_block = jnp.concatenate([head_columns(prefix_cache, 0), head_columns(prefix_cache, 1)], axis=1)
    where = jnp.stack([req_index, tok_index, kv_first]).astype(jnp.int32)
    numbers = jnp.concatenate([where, group_of, owner_order, lengths[0]])
    gains = jnp.stack([attn_gain, ffn_in_gain, ffn_out_gain])
    numbers, gains = lax.optimization_barrier((numbers, gains))
    opening = (queries, suffix_kv, jnp.stack([q_gain, k_gain]))
    attention_on = functools.partial(attention_call, numbers, across, req_count)
    shifts = range(1, across)
    every = [(line, line) for line in range(LINE)]

    def across_all(block, table, lines=every):
        return [([move(block, lines, shift)], table, shift) for shift in shifts]

    w_far, own_block = lax.optimization_barrier((w_out, own_block))
    left = move(own_block, [(0, 1), (1, 2), (2, 3)])
    right = move(own_block, [(1, 0), (2, 1), (3, 2)])
    crossed = across_all(own_block, (0, 1, 2, 3))
    plane_weights = [w_out] + [plane_shift(w_far, shift) for shift in range(1, planes)]
    state = attention_on(opening, None, [([own_block], (0, 1, 2, 3), 0)], 0)

    first = [([left], (-1, 0, 1, 2), 0), ([right], (1, 2, 3, -1), 0)] + crossed
    left, right, _ = lax.optimization_barrier((left, right, state[1]))
    onward = move(left, [(1, 2), (2, 3)])
    back = move(right, [(2, 1), (1, 0)])
    second = [([onward], (-1, -1, 0, 1), 0), ([back], (2, 3, -1, -1), 0)]
    second += across_all(pick(numbers, across, left, right), (1, 2, 1, 2))
    second += [
        ([move(block, [(0, 1), (3, 2)])], (-1, 0, 3, -1), shift) for [block], _, shift in crossed
    ]
    state = attention_on(None, state, first, 0)

    onward, back, _ = lax.optimization_barrier((onward, back, state[1]))
    far = pick(numbers, across, onward, back)
    last = move(far, [(2, 3), (1, 0)])
    third = across_all(far, (2, 3, 0, 1))
    state = attention_on(None, state, second, 0)

    last, _ = lax.optimization_barrier((last, state[1]))
    middle = last.shape[0] // 2
    table = (3, -1, -1, 0)
    fourth = []
    for [block], _, shift in third:
        halves = [move(last[:middle], [(0, 0), (3, 3)], shift), move(block[middle:], [(2, 3), (1, 0)])]
        fourth.append((halves, table, shift))
    state = attention_on(None, state, [([last], table, 0)] + third, 0)
    attention = attention_on(None, state, fourth, planes)
    plane_weights[1:], attention = lax.optimization_barrier((plane_weights[1:], attention))

    weight_parts = [[part, other_core(part)] for part in plane_weights]
    far_weights = [part for parts in weight_parts[1:] for part in parts]
    order = list(range(planes - 1, -1, -1))
    far_heads = {}
    previous = None
    for group in order:
        sent = [attention[(group + shift) % planes] for shift in range(1, planes)]
        if previous is not None:
            sent, previous = lax.optimization_barrier((sent, previous))
        previous = [plane_shift(part, shift) for shift, part in enumerate(sent, 1)]
        far_heads[group] = previous
    own_heads = [[attention[group], other_core(attention[group])] for group in range(planes)]

    def rows_of(group):
        heads_parts = list(own_heads[group])
        for part in far_heads[group]:
            heads_parts += [part, other_core(part)]
        return feed_rows(
            numbers,
            group,
            planes,
            residual,
            heads_parts,
            weight_parts[0],
            far_weights,
            gains,
            (w_gate, w_up, w_down),
        )

    keep, *send = rows_of(order[0])
    arrived = []
    for group, later in zip(order, order[1:]):
        joined = join(keep, [other_core(part) for part in send])
        own_heads[later], joined = lax.optimization_barrier((own_heads[later], joined))
        arrived.append(plane_shift(joined, group))
        keep, *send = rows_of(later)
    *send, mixed = send
    send, arrived = lax.optimization_barrier((send, arrived))
    other = [other_core(part) for part in send]
    return finish(mixed, fold(keep, arrived), other, gains)


def solution(mesh):
    in_specs = (
        P("req", "tok"),
        P("req", None),
        P("req", None),
        P(),
        P(),
        P("req", None),
        P(),
        P(),
        P("req", None),
        P("tok", None),
        P(),
        P(),
        P(),
        P(None, "tok"),
        P(None, "tok"),
        P("tok", None),
    )
    out_specs = P(("req", "tok"), None)
    return jax.shard_map(local, mesh=mesh, in_specs=in_specs, out_specs=out_specs, check_vma=False)
```

```python
import functools

import jax
import jax.numpy as jnp
from jax import lax
from jax.experimental import pallas as pl
from jax.experimental.pallas import tpu as pltpu
from jax.sharding import PartitionSpec as P

H = 8
KVH = 4
HD = 256
GROUPS = 2
EPSILON = 1e-06
MASKED = -1e30
CORES = 2
LINE = 4
NUMBERS = 3
FEED_LIMIT = 38
BF16 = jnp.bfloat16
F32 = jnp.float32
ANY = pl.BlockSpec(memory_space=pl.ANY)
VMEM = pl.BlockSpec(memory_space=pltpu.VMEM)
SMEM = pl.BlockSpec(memory_space=pltpu.SMEM)
HBM = pl.BlockSpec(memory_space=pltpu.HBM)


def mib(count):
    return count << 20


def in_vmem(values_in):
    return pltpu.with_memory_space_constraint(values_in, pltpu.VMEM)


def in_hbm(values_in):
    return pltpu.with_memory_space_constraint(values_in, pltpu.HBM)


def rms(values_in):
    return values_in * lax.rsqrt(jnp.mean(values_in * values_in, axis=-1, keepdims=True) + EPSILON)


def attend(query_ref, state, head, rows, keys, values, visible):
    max_ref, sum_ref, acc_ref = state
    columns = slice(head * HD, (head + 1) * HD)
    scores = lax.dot_general(
        query_ref[rows, columns], keys, (((1,), (1,)), ((), ())), preferred_element_type=F32
    )
    if visible is not None:
        scores = jnp.where(visible, scores, MASKED)
        block_max = jnp.max(scores, axis=1, keepdims=True)
        weights = jnp.exp(scores - block_max)
        max_ref[head, rows, :] = jnp.broadcast_to(block_max, (scores.shape[0], 128))
        sum_ref[head, rows, :] = jnp.broadcast_to(
            jnp.sum(weights, axis=1, keepdims=True), (scores.shape[0], 128)
        )
        acc_ref[rows, columns] = jnp.dot(weights.astype(BF16), values, preferred_element_type=F32)
        return
    old_max = max_ref[head, rows, :]
    new_max = jnp.maximum(old_max, jnp.max(scores, axis=1, keepdims=True))
    scale = jnp.exp(old_max - new_max)
    weights = jnp.exp(scores - new_max[:, :1])
    max_ref[head, rows, :] = new_max
    sum_ref[head, rows, :] = sum_ref[head, rows, :] * scale + jnp.sum(weights, axis=1, keepdims=True)
    acc_ref[rows, columns] = acc_ref[rows, columns] * scale[:, :1] + jnp.dot(
        weights.astype(BF16), values, preferred_element_type=F32
    )


def block_wanted(numbers, place, across, req_count):
    source_lines, col_shift = place
    per_group = req_count // GROUPS
    req_index = numbers[0]
    line = req_index // across
    source_line = jnp.int32(-1)
    for at, source in enumerate(source_lines):
        if source >= 0:
            source_line = jnp.where(line == at, source, source_line)
    source = source_line * across + lax.rem(lax.rem(req_index, across) + across - col_shift, across)
    holder = jnp.int32(-1)
    for slot in range(req_count):
        holder = jnp.where(numbers[NUMBERS + req_count + slot] == source, slot // per_group, holder)
    return (source_line >= 0) & (holder == numbers[NUMBERS + req_index])


def attention_kernel(places, counts, across, req_count, heads, first, parts, near, *refs):
    refs = list(refs)
    take = lambda count: [refs.pop(0) for _ in range(count)]
    (numbers,) = take(1)
    if first:
        queries_ref, suffix, gains = take(3)
    else:
        query_ref, max_in, sum_in, acc_in = take(4)
    blocks = [take(count) for count in counts]
    take(near)
    if first:
        query_ref, max_ref, sum_ref, acc_ref, queries, own_keys, own_values, held, sems, own_sems = refs
    elif parts:
        out_refs = take(parts)
        max_ref, sum_ref, acc_ref, held, sems = refs
    else:
        max_ref, sum_ref, acc_ref = take(3)
        held, sems = refs
    state = (max_ref, sum_ref, acc_ref)
    wanted = [block_wanted(numbers, place, across, req_count) for place in places]

    def copies_of(at):
        extent = held.shape[1] // counts[at]
        return [
            pltpu.make_async_copy(
                block, held.at[at, pl.ds(piece * extent, extent)], sems.at[at, piece]
            )
            for piece, block in enumerate(blocks[at])
        ]

    for at in range(len(places)):

        @pl.when(wanted[at])
        def _():
            for copy in copies_of(at):
                copy.start()

    row_count = query_ref.shape[0]
    step = min(256, row_count)
    if first:
        begin = pl.multiple_of(numbers[2] * HD, HD)
        copies = [pltpu.make_async_copy(queries_ref, queries, own_sems.at[2])] + [
            pltpu.make_async_copy(
                suffix.at[:, pl.ds(pl.multiple_of(begin + which * KVH * HD, HD), HD)],
                target,
                own_sems.at[which],
            )
            for which, target in enumerate((own_keys, own_values))
        ]
        for copy in copies:
            copy.start()
        copies[0].wait()
        for head in range(heads):
            columns = slice(head * HD, (head + 1) * HD)
            normed = (rms(queries[:, columns].astype(F32)) * gains[:1, :]).astype(BF16)
            query_ref[:, columns] = normed * jnp.asarray(HD ** (-0.5), BF16)
        for copy in copies[1:]:
            copy.wait()
        own_keys[...] = (rms(own_keys[...].astype(F32)) * gains[1:, :]).astype(BF16)
        ends = []
        first_length = NUMBERS + 2 * req_count
        for at in range(first_length, numbers.shape[0] - 1):
            ends.append(numbers[at] + (ends[-1] if ends else 0))
        for begin in range(0, row_count, step):
            rows = slice(begin, begin + step)
            seen = begin + step
            row_at = lax.broadcasted_iota(jnp.int32, (step, seen), 0) + begin
            key_at = lax.broadcasted_iota(jnp.int32, (step, seen), 1)
            visible = key_at <= row_at
            for end in ends:
                visible &= (row_at < end) | (key_at >= end)
            for head in range(heads):
                attend(query_ref, state, head, rows, own_keys[:seen, :], own_values[:seen, :], visible)
    else:
        max_ref[...] = max_in[...]
        sum_ref[...] = sum_in[...]
        acc_ref[...] = acc_in[...]

    for at in range(len(places)):

        @pl.when(wanted[at])
        def _():
            for copy in copies_of(at):
                copy.wait()

            @pl.loop(0, row_count // step)
            def _(turn):
                rows = pl.ds(pl.multiple_of(turn * step, step), step)
                for head in range(heads):
                    attend(query_ref, state, head, rows, held[at, :, :HD], held[at, :, HD:], None)


    for at in range(parts):
        extent = row_count // parts
        begin = lax.rem(numbers[1] // CORES + at, parts) * extent
        rows = pl.ds(pl.multiple_of(begin, extent), extent)
        for head in range(heads):
            columns = slice(head * HD, (head + 1) * HD)
            out_refs[at][:, columns] = (acc_ref[rows, columns] / sum_ref[head, rows, :1]).astype(BF16)


def attention_call(numbers, across, req_count, opening, state, wave, parts, near=()):
    blocks = [block for parts_of, _, _ in wave for block in parts_of]
    counts = [len(parts_of) for parts_of, _, _ in wave]
    places = [(sources, shift) for _, sources, shift in wave]
    query = opening[0] if state is None else state[0]
    row_count = query.shape[0]
    heads = query.shape[1] // HD
    shapes = [
        ((heads, row_count, 128), F32),
        ((heads, row_count, 128), F32),
        ((row_count, heads * HD), F32),
    ]
    first = state is None
    kernel = functools.partial(attention_kernel, places, counts, across, req_count, heads, first, parts, len(near))
    if first:
        queries, suffix, gains = opening
        operands = (numbers, in_hbm(queries), in_hbm(suffix), gains, *blocks)
        in_specs = [SMEM, HBM, HBM, VMEM] + [ANY] * len(blocks)
    else:
        operands = (numbers, *state, *blocks, *[in_vmem(part) for part in near])
        in_specs = [SMEM] + [VMEM] * 4 + [ANY] * len(blocks) + [VMEM] * len(near)
    scratch = [
        pltpu.VMEM((len(wave), row_count, 2 * HD), BF16),
        pltpu.SemaphoreType.DMA((len(wave), 2)),
    ]
    states = [jax.ShapeDtypeStruct(shape, dtype) for shape, dtype in shapes]
    if first:
        out_shape = [jax.ShapeDtypeStruct(query.shape, BF16)] + states
        scratch = (
            [pltpu.VMEM(query.shape, BF16)]
            + [pltpu.VMEM((row_count, HD), BF16)] * 2
            + scratch
            + [pltpu.SemaphoreType.DMA((3,))]
        )
    elif parts:
        out_shape = [jax.ShapeDtypeStruct((row_count // parts, query.shape[1]), BF16)] * parts
        scratch = [pltpu.VMEM(shape, dtype) for shape, dtype in shapes] + scratch
    else:
        out_shape = states
    result = pl.pallas_call(
        kernel,
        in_specs=in_specs,
        out_specs=[VMEM] * len(out_shape),
        out_shape=out_shape,
        scratch_shapes=scratch,
        compiler_params=pltpu.CompilerParams(vmem_limit_bytes=mib(7)),
        cost_estimate=pl.CostEstimate(
            flops=8 * row_count * row_count * heads * HD,
            bytes_accessed=mib(4),
            transcendentals=2 * row_count * row_count * heads,
        ),
        name="attend_blocks",
    )(*operands)
    return result if first or parts else [query, *result]


def pick_kernel(lines, numbers, upper_ref, lower_ref, out_ref):
    upper = numbers[0] >= lines

    @pl.when(upper)
    def _():
        out_ref[...] = upper_ref[...]

    @pl.when(jnp.logical_not(upper))
    def _():
        out_ref[...] = lower_ref[...]


def pick(numbers, across, upper, lower):
    return pl.pallas_call(
        functools.partial(pick_kernel, across * LINE // 2),
        in_specs=[SMEM, VMEM, VMEM],
        out_specs=VMEM,
        out_shape=jax.ShapeDtypeStruct(upper.shape, upper.dtype),
        compiler_params=pltpu.CompilerParams(vmem_limit_bytes=mib(4)),
        name="pick",
    )(numbers, upper, lower)


def column_step(width):
    return 512 if width % 512 == 0 else 128


def feed_kernel(pieces, group, planes, *refs):
    refs = list(refs)
    take = lambda count: [refs.pop(0) for _ in range(count)]
    (numbers,), heads_refs, (gains,) = take(1), take(pieces), take(1)
    (gate_ref,), weight_refs = take(1), take(pieces - 2)
    up_source, down_source, residual_ref, *near_sources = take(5)
    (keep_ref, *send_refs), mixed_refs = take(3), take(int(group == 0))
    spare, total_ref, normed_ref, up_ref, down_ref, sems = refs
    share, width = keep_ref.shape
    hidden = gate_ref.shape[1]
    core_at = lax.rem(numbers[1], CORES)
    first_row = lax.rem(numbers[1] // CORES + group, planes) * CORES * share
    unroll = 5
    step = 512 if hidden % 512 == 0 else 256

    def columns_of(at, extent):
        return pl.ds(at * extent if isinstance(at, int) else pl.multiple_of(at * extent, extent), extent)

    residual_copies = []
    for tile in range(CORES):
        target = pl.multiple_of(jnp.where(core_at == tile, 0, share), share)
        residual_copies.append(
            pltpu.make_async_copy(
                residual_ref.at[pl.ds(pl.multiple_of(first_row + tile * share, share), share)],
                spare.at[pl.ds(target, share), pl.ds(0, width)],
                sems.at[tile],
            )
        )
    depth = near_sources[0].shape[0]
    near_copies = [
        pltpu.make_async_copy(source, down_ref.at[pl.ds(at * depth, depth)], sems.at[CORES + at])
        for at, source in enumerate(near_sources)
    ]
    down_copies = [
        pltpu.make_async_copy(down_source.at[rows], down_ref.at[rows], sems.at[CORES + 2 + at])
        for at, rows in enumerate((pl.ds(0, 2 * depth), pl.ds(2 * depth, hidden - 2 * depth)))
    ]
    up_copies = [
        pltpu.make_async_copy(
            up_source.at[:, pl.ds(begin, step)], up_ref.at[:, pl.ds(begin, step)], sems.at[CORES + 4 + at]
        )
        for at, begin in enumerate(range(0, hidden, step))
    ]
    for copy in [*near_copies, *residual_copies, *up_copies, down_copies[1]]:
        copy.start()
    wide = column_step(width)

    @pl.loop(0, width // wide)
    def _(at):
        columns = columns_of(at, wide)
        total = jnp.dot(heads_refs[2][...], weight_refs[0][:, columns], preferred_element_type=F32)
        for piece in range(3, pieces):
            total += jnp.dot(
                heads_refs[piece][...], weight_refs[piece - 2][:, columns], preferred_element_type=F32
            )
        total_ref[:, columns] = total

    for copy in near_copies:
        copy.wait()

    @pl.loop(0, width // wide)
    def _(at):
        columns = columns_of(at, wide)
        total = total_ref[:, columns]
        for piece in range(2):
            total += jnp.dot(
                heads_refs[piece][...],
                down_ref[piece * depth : (piece + 1) * depth, columns],
                preferred_element_type=F32,
            )
        total_ref[:, columns] = total

    down_copies[0].start()
    for copy in residual_copies:
        copy.wait()
    extent = min(64, share)

    @pl.loop(0, CORES * share // extent)
    def _(at):
        rows = pl.ds(pl.multiple_of(at * extent, extent), extent)
        source = lax.rem(at * extent + core_at * share, CORES * share)
        total = total_ref[pl.ds(pl.multiple_of(source, extent), extent), :]
        mixed = spare[rows, :width].astype(F32) + rms(total) * gains[0:1, :]
        normed_ref[rows, :] = (rms(mixed) * gains[1:2, :]).astype(BF16)
        for mixed_ref in mixed_refs:

            @pl.when(at < share // extent)
            def _():
                mixed_ref[rows, :] = mixed

    for at, copy in enumerate(up_copies):
        columns = slice(at * step, (at + 1) * step)
        gate = jnp.dot(normed_ref[...], gate_ref[:, columns], preferred_element_type=F32)
        copy.wait()
        upward = jnp.dot(normed_ref[...], up_ref[:, columns], preferred_element_type=F32)
        spare[:, columns] = (jax.nn.gelu(gate, approximate=True) * upward).astype(BF16)

    for copy in down_copies:
        copy.wait()

    @pl.loop(0, width // step, unroll=unroll)
    def _(at):
        columns = columns_of(at, step)
        down = jnp.dot(spare[:, :hidden], down_ref[:, columns], preferred_element_type=F32)
        keep_ref[:, columns] = down[:share]
        for at_send, send_ref in enumerate(send_refs):
            begin = share + at_send * send_ref.shape[0]
            send_ref[:, columns] = down[begin : begin + send_ref.shape[0]].astype(BF16)


def feed_rows(
    numbers, group, planes, residual, heads_parts, near_weights, far_weights, gains, feed_weights
):
    pieces = len(heads_parts)
    rows, depth = heads_parts[0].shape
    width = residual.shape[1]
    share = rows // CORES
    hidden = feed_weights[0].shape[1]
    return pl.pallas_call(
        functools.partial(feed_kernel, pieces, group, planes),
        in_specs=[SMEM] + [VMEM] * (2 * pieces) + [HBM] * 5,
        out_specs=[VMEM] * (3 + (group == 0)),
        out_shape=[pltpu.VMEM((share, width), F32)]
        + [pltpu.VMEM((share // 2, width), BF16)] * 2
        + [pltpu.VMEM((share, width), F32)] * (group == 0),
        scratch_shapes=[
            pltpu.VMEM((rows, max(width, hidden)), BF16),
            pltpu.VMEM((rows, width), F32),
            pltpu.VMEM((rows, width), BF16),
            pltpu.VMEM((width, hidden), BF16),
            pltpu.VMEM((hidden, width), BF16),
            pltpu.SemaphoreType.DMA((CORES + 4 + hidden // 256,)),
        ],
        compiler_params=pltpu.CompilerParams(vmem_limit_bytes=mib(FEED_LIMIT)),
        cost_estimate=pl.CostEstimate(
            flops=2 * rows * width * (pieces * heads_parts[0].shape[1] + 3 * hidden),
            bytes_accessed=mib(16),
            transcendentals=rows * hidden,
        ),
        name="feed_rows",
    )(
        numbers,
        *heads_parts,
        gains,
        *[in_vmem(part) for part in (feed_weights[0], *far_weights)],
        *[in_hbm(part) for part in (*feed_weights[1:], residual, *near_weights)],
    )


def join_kernel(keep_ref, *refs):
    out_ref = refs[-1]
    half = keep_ref.shape[0] // 2
    for at in range(2):
        rows = slice(at * half, (at + 1) * half)
        out_ref[rows, :] = (keep_ref[rows, :] + refs[at][...].astype(F32)).astype(BF16)


def join(keep, other):
    return pl.pallas_call(
        join_kernel,
        out_shape=jax.ShapeDtypeStruct(keep.shape, BF16),
        compiler_params=pltpu.CompilerParams(vmem_limit_bytes=mib(8)),
        name="join",
    )(keep, *other)


def fold_kernel(keep_ref, *refs):
    total = keep_ref[...]
    for other in refs[:-1]:
        total = total + other[...].astype(F32)
    refs[-1][...] = total


def fold(keep, arrived):
    return pl.pallas_call(
        fold_kernel,
        out_shape=jax.ShapeDtypeStruct(keep.shape, F32),
        compiler_params=pltpu.CompilerParams(vmem_limit_bytes=mib(7)),
        name="fold",
    )(keep, *arrived)


def finish_kernel(mixed_ref, total_ref, *refs):
    gains_ref, out_ref = refs[-2:]
    half = total_ref.shape[0] // 2
    for at in range(2):
        rows = slice(at * half, (at + 1) * half)
        total = total_ref[rows, :] + refs[at][...].astype(F32)
        out_ref[rows, :] = (mixed_ref[rows, :] + rms(total) * gains_ref[2:3, :]).astype(BF16)


def finish(mixed, total, other, gains):
    return pl.pallas_call(
        finish_kernel,
        out_shape=jax.ShapeDtypeStruct(mixed.shape, BF16),
        compiler_params=pltpu.CompilerParams(vmem_limit_bytes=mib(7)),
        name="finish",
    )(mixed, total, *other, gains)


def local(
    queries,
    suffix_kv,
    prefix_cache,
    q_gain,
    k_gain,
    lengths,
    group_of,
    owner_order,
    residual,
    w_out,
    attn_gain,
    ffn_in_gain,
    ffn_out_gain,
    w_gate,
    w_up,
    w_down,
):
    req_count = lax.axis_size("req")
    tok_count = lax.axis_size("tok")
    req_index = lax.axis_index("req")
    tok_index = lax.axis_index("tok")
    across = req_count // LINE
    planes = tok_count // CORES
    row_count = queries.shape[0]
    share = row_count // tok_count
    heads_here = queries.shape[1] // HD
    head_ratio = H // KVH
    kv_first = tok_index * heads_here // head_ratio
    kv_width = KVH * HD

    def head_columns(rows_in, which):
        return lax.dynamic_slice_in_dim(rows_in, which * kv_width + kv_first * HD, HD, 1)

    def move(values_in, lines, shift=0):
        pairs = [
            (source * across + col, target * across + (col + shift) % across)
            for source, target in lines
            for col in range(across)
        ]
        return lax.ppermute(values_in, "req", pairs)

    def other_core(values_in):
        return lax.ppermute(values_in, "tok", [(at, at ^ 1) for at in range(tok_count)])

    def plane_shift(values_in, shift):
        return lax.ppermute(
            values_in, "tok", [(at, (at + CORES * shift) % tok_count) for at in range(tok_count)]
        )

    own_block = jnp.concatenate([head_columns(prefix_cache, 0), head_columns(prefix_cache, 1)], axis=1)
    where = jnp.stack([req_index, tok_index, kv_first]).astype(jnp.int32)
    numbers = jnp.concatenate([where, group_of, owner_order, lengths[0]])
    gains = jnp.stack([attn_gain, ffn_in_gain, ffn_out_gain])
    numbers, gains = lax.optimization_barrier((numbers, gains))
    opening = (queries, suffix_kv, jnp.stack([q_gain, k_gain]))
    attention_on = functools.partial(attention_call, numbers, across, req_count)
    shifts = range(1, across)
    every = [(line, line) for line in range(LINE)]

    def across_all(block, table, lines=every):
        return [([move(block, lines, shift)], table, shift) for shift in shifts]

    w_far, own_block = lax.optimization_barrier((w_out, own_block))
    left = move(own_block, [(0, 1), (1, 2), (2, 3)])
    right = move(own_block, [(1, 0), (2, 1), (3, 2)])
    crossed = across_all(own_block, (0, 1, 2, 3))
    plane_weights = [w_out] + [plane_shift(w_far, shift) for shift in range(1, planes)]
    state = attention_on(opening, None, [([own_block], (0, 1, 2, 3), 0)], 0)

    first = [([left], (-1, 0, 1, 2), 0), ([right], (1, 2, 3, -1), 0)] + crossed
    left, right, _ = lax.optimization_barrier((left, right, state[1]))
    onward = move(left, [(1, 2), (2, 3)])
    back = move(right, [(2, 1), (1, 0)])
    second = [([onward], (-1, -1, 0, 1), 0), ([back], (2, 3, -1, -1), 0)]
    second += across_all(pick(numbers, across, left, right), (1, 2, 1, 2))
    second += [
        ([move(block, [(0, 1), (3, 2)])], (-1, 0, 3, -1), shift) for [block], _, shift in crossed
    ]
    state = attention_on(None, state, first, 0)

    onward, back, _ = lax.optimization_barrier((onward, back, state[1]))
    far = pick(numbers, across, onward, back)
    last = move(far, [(2, 3), (1, 0)])
    third = across_all(far, (2, 3, 0, 1))
    state = attention_on(None, state, second, 0)

    last, _ = lax.optimization_barrier((last, state[1]))
    middle = last.shape[0] // 2
    table = (3, -1, -1, 0)
    fourth = []
    for [block], _, shift in third:
        halves = [move(last[:middle], [(0, 0), (3, 3)], shift), move(block[middle:], [(2, 3), (1, 0)])]
        fourth.append((halves, table, shift))
    state = attention_on(None, state, [([last], table, 0)] + third, 0)
    attention = attention_on(None, state, fourth, planes)
    plane_weights[1:], attention = lax.optimization_barrier((plane_weights[1:], attention))

    weight_parts = [[part, other_core(part)] for part in plane_weights]
    far_weights = [part for parts in weight_parts[1:] for part in parts]
    order = list(range(planes - 1, -1, -1))
    far_heads = {}
    previous = None
    for group in order:
        sent = [attention[(group + shift) % planes] for shift in range(1, planes)]
        if previous is not None:
            sent, previous = lax.optimization_barrier((sent, previous))
        previous = [plane_shift(part, shift) for shift, part in enumerate(sent, 1)]
        far_heads[group] = previous
    own_heads = [[attention[group], other_core(attention[group])] for group in range(planes)]

    def rows_of(group):
        heads_parts = list(own_heads[group])
        for part in far_heads[group]:
            heads_parts += [part, other_core(part)]
        return feed_rows(
            numbers,
            group,
            planes,
            residual,
            heads_parts,
            weight_parts[0],
            far_weights,
            gains,
            (w_gate, w_up, w_down),
        )

    keep, *send = rows_of(order[0])
    arrived = []
    for group, later in zip(order, order[1:]):
        joined = join(keep, [other_core(part) for part in send])
        own_heads[later], joined = lax.optimization_barrier((own_heads[later], joined))
        arrived.append(plane_shift(joined, group))
        keep, *send = rows_of(later)
    *send, mixed = send
    send, arrived = lax.optimization_barrier((send, arrived))
    other = [other_core(part) for part in send]
    return finish(mixed, fold(keep, arrived), other, gains)


def solution(mesh):
    in_specs = (
        P("req", "tok"),
        P("req", None),
        P("req", None),
        P(),
        P(),
        P("req", None),
        P(),
        P(),
        P("req", None),
        P("tok", None),
        P(),
        P(),
        P(),
        P(None, "tok"),
        P(None, "tok"),
        P("tok", None),
    )
    out_specs = P(("req", "tok"), None)
    return jax.shard_map(local, mesh=mesh, in_specs=in_specs, out_specs=out_specs, check_vma=False)
```

```python
import functools

import jax
import jax.numpy as jnp
from jax import lax
from jax.experimental import pallas as pl
from jax.experimental.pallas import tpu as pltpu
from jax.sharding import PartitionSpec as P

H = 8
KVH = 4
HD = 256
GROUPS = 2
EPSILON = 1e-06
MASKED = -1e30
CORES = 2
LINE = 4
NUMBERS = 3
FEED_LIMIT = 38
BF16 = jnp.bfloat16
F32 = jnp.float32
ANY = pl.BlockSpec(memory_space=pl.ANY)
VMEM = pl.BlockSpec(memory_space=pltpu.VMEM)
SMEM = pl.BlockSpec(memory_space=pltpu.SMEM)
HBM = pl.BlockSpec(memory_space=pltpu.HBM)


def mib(count):
    return count << 20


def in_vmem(values_in):
    return pltpu.with_memory_space_constraint(values_in, pltpu.VMEM)


def in_hbm(values_in):
    return pltpu.with_memory_space_constraint(values_in, pltpu.HBM)


def rms(values_in):
    return values_in * lax.rsqrt(jnp.mean(values_in * values_in, axis=-1, keepdims=True) + EPSILON)


def attend(query_ref, state, head, rows, keys, values, visible):
    max_ref, sum_ref, acc_ref = state
    columns = slice(head * HD, (head + 1) * HD)
    scores = lax.dot_general(
        query_ref[rows, columns], keys, (((1,), (1,)), ((), ())), preferred_element_type=F32
    )
    if visible is not None:
        scores = jnp.where(visible, scores, MASKED)
        block_max = jnp.max(scores, axis=1, keepdims=True)
        weights = jnp.exp(scores - block_max)
        max_ref[head, rows, :] = jnp.broadcast_to(block_max, (scores.shape[0], 128))
        sum_ref[head, rows, :] = jnp.broadcast_to(
            jnp.sum(weights, axis=1, keepdims=True), (scores.shape[0], 128)
        )
        acc_ref[rows, columns] = jnp.dot(weights.astype(BF16), values, preferred_element_type=F32)
        return
    old_max = max_ref[head, rows, :]
    new_max = jnp.maximum(old_max, jnp.max(scores, axis=1, keepdims=True))
    scale = jnp.exp(old_max - new_max)
    weights = jnp.exp(scores - new_max[:, :1])
    max_ref[head, rows, :] = new_max
    sum_ref[head, rows, :] = sum_ref[head, rows, :] * scale + jnp.sum(weights, axis=1, keepdims=True)
    acc_ref[rows, columns] = acc_ref[rows, columns] * scale[:, :1] + jnp.dot(
        weights.astype(BF16), values, preferred_element_type=F32
    )


def block_wanted(numbers, place, across, req_count):
    source_lines, col_shift = place
    per_group = req_count // GROUPS
    req_index = numbers[0]
    line = req_index // across
    source_line = jnp.int32(-1)
    for at, source in enumerate(source_lines):
        if source >= 0:
            source_line = jnp.where(line == at, source, source_line)
    source = source_line * across + lax.rem(lax.rem(req_index, across) + across - col_shift, across)
    holder = jnp.int32(-1)
    for slot in range(req_count):
        holder = jnp.where(numbers[NUMBERS + req_count + slot] == source, slot // per_group, holder)
    return (source_line >= 0) & (holder == numbers[NUMBERS + req_index])


def attention_kernel(places, counts, across, req_count, heads, first, parts, near, *refs):
    refs = list(refs)
    take = lambda count: [refs.pop(0) for _ in range(count)]
    (numbers,) = take(1)
    if first:
        queries_ref, suffix, gains = take(3)
    else:
        query_ref, max_in, sum_in, acc_in = take(4)
    blocks = [take(count) for count in counts]
    take(near)
    if first:
        query_ref, max_ref, sum_ref, acc_ref, queries, own_keys, own_values, held, sems, own_sems = refs
    elif parts:
        out_refs = take(parts)
        max_ref, sum_ref, acc_ref, held, sems = refs
    else:
        max_ref, sum_ref, acc_ref = take(3)
        held, sems = refs
    state = (max_ref, sum_ref, acc_ref)
    wanted = [block_wanted(numbers, place, across, req_count) for place in places]

    def copies_of(at):
        extent = held.shape[1] // counts[at]
        return [
            pltpu.make_async_copy(
                block, held.at[at, pl.ds(piece * extent, extent)], sems.at[at, piece]
            )
            for piece, block in enumerate(blocks[at])
        ]

    for at in range(len(places)):

        @pl.when(wanted[at])
        def _():
            for copy in copies_of(at):
                copy.start()

    row_count = query_ref.shape[0]
    step = min(256, row_count)
    if first:
        begin = pl.multiple_of(numbers[2] * HD, HD)
        copies = [pltpu.make_async_copy(queries_ref, queries, own_sems.at[2])] + [
            pltpu.make_async_copy(
                suffix.at[:, pl.ds(pl.multiple_of(begin + which * KVH * HD, HD), HD)],
                target,
                own_sems.at[which],
            )
            for which, target in enumerate((own_keys, own_values))
        ]
        for copy in copies:
            copy.start()
        copies[0].wait()
        for head in range(heads):
            columns = slice(head * HD, (head + 1) * HD)
            normed = (rms(queries[:, columns].astype(F32)) * gains[:1, :]).astype(BF16)
            query_ref[:, columns] = normed * jnp.asarray(HD ** (-0.5), BF16)
        for copy in copies[1:]:
            copy.wait()
        own_keys[...] = (rms(own_keys[...].astype(F32)) * gains[1:, :]).astype(BF16)
        ends = []
        first_length = NUMBERS + 2 * req_count
        for at in range(first_length, numbers.shape[0] - 1):
            ends.append(numbers[at] + (ends[-1] if ends else 0))
        for begin in range(0, row_count, step):
            rows = slice(begin, begin + step)
            seen = begin + step
            row_at = lax.broadcasted_iota(jnp.int32, (step, seen), 0) + begin
            key_at = lax.broadcasted_iota(jnp.int32, (step, seen), 1)
            visible = key_at <= row_at
            for end in ends:
                visible &= (row_at < end) | (key_at >= end)
            for head in range(heads):
                attend(query_ref, state, head, rows, own_keys[:seen, :], own_values[:seen, :], visible)
    else:
        max_ref[...] = max_in[...]
        sum_ref[...] = sum_in[...]
        acc_ref[...] = acc_in[...]

    for at in range(len(places)):

        @pl.when(wanted[at])
        def _():
            for copy in copies_of(at):
                copy.wait()

            @pl.loop(0, row_count // step)
            def _(turn):
                rows = pl.ds(pl.multiple_of(turn * step, step), step)
                for head in range(heads):
                    attend(query_ref, state, head, rows, held[at, :, :HD], held[at, :, HD:], None)


    for at in range(parts):
        extent = row_count // parts
        begin = lax.rem(numbers[1] // CORES + at, parts) * extent
        rows = pl.ds(pl.multiple_of(begin, extent), extent)
        for head in range(heads):
            columns = slice(head * HD, (head + 1) * HD)
            out_refs[at][:, columns] = (acc_ref[rows, columns] / sum_ref[head, rows, :1]).astype(BF16)


def attention_call(numbers, across, req_count, opening, state, wave, parts, near=()):
    blocks = [block for parts_of, _, _ in wave for block in parts_of]
    counts = [len(parts_of) for parts_of, _, _ in wave]
    places = [(sources, shift) for _, sources, shift in wave]
    query = opening[0] if state is None else state[0]
    row_count = query.shape[0]
    heads = query.shape[1] // HD
    shapes = [
        ((heads, row_count, 128), F32),
        ((heads, row_count, 128), F32),
        ((row_count, heads * HD), F32),
    ]
    first = state is None
    kernel = functools.partial(attention_kernel, places, counts, across, req_count, heads, first, parts, len(near))
    if first:
        queries, suffix, gains = opening
        operands = (numbers, in_hbm(queries), in_hbm(suffix), gains, *blocks)
        in_specs = [SMEM, HBM, HBM, VMEM] + [ANY] * len(blocks)
    else:
        operands = (numbers, *state, *blocks, *[in_vmem(part) for part in near])
        in_specs = [SMEM] + [VMEM] * 4 + [ANY] * len(blocks) + [VMEM] * len(near)
    scratch = [
        pltpu.VMEM((len(wave), row_count, 2 * HD), BF16),
        pltpu.SemaphoreType.DMA((len(wave), 2)),
    ]
    states = [jax.ShapeDtypeStruct(shape, dtype) for shape, dtype in shapes]
    if first:
        out_shape = [jax.ShapeDtypeStruct(query.shape, BF16)] + states
        scratch = (
            [pltpu.VMEM(query.shape, BF16)]
            + [pltpu.VMEM((row_count, HD), BF16)] * 2
            + scratch
            + [pltpu.SemaphoreType.DMA((3,))]
        )
    elif parts:
        out_shape = [jax.ShapeDtypeStruct((row_count // parts, query.shape[1]), BF16)] * parts
        scratch = [pltpu.VMEM(shape, dtype) for shape, dtype in shapes] + scratch
    else:
        out_shape = states
    result = pl.pallas_call(
        kernel,
        in_specs=in_specs,
        out_specs=[VMEM] * len(out_shape),
        out_shape=out_shape,
        scratch_shapes=scratch,
        compiler_params=pltpu.CompilerParams(vmem_limit_bytes=mib(7)),
        cost_estimate=pl.CostEstimate(
            flops=8 * row_count * row_count * heads * HD,
            bytes_accessed=mib(4),
            transcendentals=2 * row_count * row_count * heads,
        ),
        name="attend_blocks",
    )(*operands)
    return result if first or parts else [query, *result]


def pick_kernel(lines, numbers, upper_ref, lower_ref, out_ref):
    upper = numbers[0] >= lines

    @pl.when(upper)
    def _():
        out_ref[...] = upper_ref[...]

    @pl.when(jnp.logical_not(upper))
    def _():
        out_ref[...] = lower_ref[...]


def pick(numbers, across, upper, lower):
    return pl.pallas_call(
        functools.partial(pick_kernel, across * LINE // 2),
        in_specs=[SMEM, VMEM, VMEM],
        out_specs=VMEM,
        out_shape=jax.ShapeDtypeStruct(upper.shape, upper.dtype),
        compiler_params=pltpu.CompilerParams(vmem_limit_bytes=mib(4)),
        name="pick",
    )(numbers, upper, lower)


def column_step(width):
    return 512 if width % 512 == 0 else 128


def feed_kernel(pieces, group, planes, *refs):
    refs = list(refs)
    take = lambda count: [refs.pop(0) for _ in range(count)]
    (numbers,), heads_refs, (gains,) = take(1), take(pieces), take(1)
    (gate_ref,), weight_refs = take(1), take(pieces - 2)
    up_source, down_source, residual_ref, *near_sources = take(5)
    (keep_ref, *send_refs), mixed_refs = take(3), take(int(group == 0))
    spare, total_ref, normed_ref, up_ref, down_ref, sems = refs
    share, width = keep_ref.shape
    hidden = gate_ref.shape[1]
    core_at = lax.rem(numbers[1], CORES)
    first_row = lax.rem(numbers[1] // CORES + group, planes) * CORES * share
    unroll = 5
    step = 512 if hidden % 512 == 0 else 256

    def columns_of(at, extent):
        return pl.ds(at * extent if isinstance(at, int) else pl.multiple_of(at * extent, extent), extent)

    residual_copies = []
    for tile in range(CORES):
        target = pl.multiple_of(jnp.where(core_at == tile, 0, share), share)
        residual_copies.append(
            pltpu.make_async_copy(
                residual_ref.at[pl.ds(pl.multiple_of(first_row + tile * share, share), share)],
                spare.at[pl.ds(target, share), pl.ds(0, width)],
                sems.at[tile],
            )
        )
    depth = near_sources[0].shape[0]
    near_copies = [
        pltpu.make_async_copy(source, down_ref.at[pl.ds(at * depth, depth)], sems.at[CORES + at])
        for at, source in enumerate(near_sources)
    ]
    down_copies = [
        pltpu.make_async_copy(down_source.at[rows], down_ref.at[rows], sems.at[CORES + 2 + at])
        for at, rows in enumerate((pl.ds(0, 2 * depth), pl.ds(2 * depth, hidden - 2 * depth)))
    ]
    up_copies = [
        pltpu.make_async_copy(
            up_source.at[:, pl.ds(begin, step)], up_ref.at[:, pl.ds(begin, step)], sems.at[CORES + 4 + at]
        )
        for at, begin in enumerate(range(0, hidden, step))
    ]
    for copy in [*near_copies, *residual_copies, *up_copies, down_copies[1]]:
        copy.start()
    wide = column_step(width)

    @pl.loop(0, width // wide, unroll=5)
    def _(at):
        columns = columns_of(at, wide)
        total = jnp.dot(heads_refs[2][...], weight_refs[0][:, columns], preferred_element_type=F32)
        for piece in range(3, pieces):
            total += jnp.dot(
                heads_refs[piece][...], weight_refs[piece - 2][:, columns], preferred_element_type=F32
            )
        total_ref[:, columns] = total

    for copy in near_copies:
        copy.wait()

    @pl.loop(0, width // wide, unroll=5)
    def _(at):
        columns = columns_of(at, wide)
        total = total_ref[:, columns]
        for piece in range(2):
            total += jnp.dot(
                heads_refs[piece][...],
                down_ref[piece * depth : (piece + 1) * depth, columns],
                preferred_element_type=F32,
            )
        total_ref[:, columns] = total

    down_copies[0].start()
    for copy in residual_copies:
        copy.wait()
    extent = min(64, share)

    @pl.loop(0, CORES * share // extent)
    def _(at):
        rows = pl.ds(pl.multiple_of(at * extent, extent), extent)
        source = lax.rem(at * extent + core_at * share, CORES * share)
        total = total_ref[pl.ds(pl.multiple_of(source, extent), extent), :]
        mixed = spare[rows, :width].astype(F32) + rms(total) * gains[0:1, :]
        normed_ref[rows, :] = (rms(mixed) * gains[1:2, :]).astype(BF16)
        for mixed_ref in mixed_refs:

            @pl.when(at < share // extent)
            def _():
                mixed_ref[rows, :] = mixed

    for at, copy in enumerate(up_copies):
        columns = slice(at * step, (at + 1) * step)
        gate = jnp.dot(normed_ref[...], gate_ref[:, columns], preferred_element_type=F32)
        copy.wait()
        upward = jnp.dot(normed_ref[...], up_ref[:, columns], preferred_element_type=F32)
        spare[:, columns] = (jax.nn.gelu(gate, approximate=True) * upward).astype(BF16)

    for copy in down_copies:
        copy.wait()

    @pl.loop(0, width // step, unroll=unroll)
    def _(at):
        columns = columns_of(at, step)
        down = jnp.dot(spare[:, :hidden], down_ref[:, columns], preferred_element_type=F32)
        keep_ref[:, columns] = down[:share]
        for at_send, send_ref in enumerate(send_refs):
            begin = share + at_send * send_ref.shape[0]
            send_ref[:, columns] = down[begin : begin + send_ref.shape[0]].astype(BF16)


def feed_rows(
    numbers, group, planes, residual, heads_parts, near_weights, far_weights, gains, feed_weights
):
    pieces = len(heads_parts)
    rows, depth = heads_parts[0].shape
    width = residual.shape[1]
    share = rows // CORES
    hidden = feed_weights[0].shape[1]
    return pl.pallas_call(
        functools.partial(feed_kernel, pieces, group, planes),
        in_specs=[SMEM] + [VMEM] * (2 * pieces) + [HBM] * 5,
        out_specs=[VMEM] * (3 + (group == 0)),
        out_shape=[pltpu.VMEM((share, width), F32)]
        + [pltpu.VMEM((share // 2, width), BF16)] * 2
        + [pltpu.VMEM((share, width), F32)] * (group == 0),
        scratch_shapes=[
            pltpu.VMEM((rows, max(width, hidden)), BF16),
            pltpu.VMEM((rows, width), F32),
            pltpu.VMEM((rows, width), BF16),
            pltpu.VMEM((width, hidden), BF16),
            pltpu.VMEM((hidden, width), BF16),
            pltpu.SemaphoreType.DMA((CORES + 4 + hidden // 256,)),
        ],
        compiler_params=pltpu.CompilerParams(vmem_limit_bytes=mib(FEED_LIMIT)),
        cost_estimate=pl.CostEstimate(
            flops=2 * rows * width * (pieces * heads_parts[0].shape[1] + 3 * hidden),
            bytes_accessed=mib(16),
            transcendentals=rows * hidden,
        ),
        name="feed_rows",
    )(
        numbers,
        *heads_parts,
        gains,
        *[in_vmem(part) for part in (feed_weights[0], *far_weights)],
        *[in_hbm(part) for part in (*feed_weights[1:], residual, *near_weights)],
    )


def join_kernel(keep_ref, *refs):
    out_ref = refs[-1]
    half = keep_ref.shape[0] // 2
    for at in range(2):
        rows = slice(at * half, (at + 1) * half)
        out_ref[rows, :] = (keep_ref[rows, :] + refs[at][...].astype(F32)).astype(BF16)


def join(keep, other):
    return pl.pallas_call(
        join_kernel,
        out_shape=jax.ShapeDtypeStruct(keep.shape, BF16),
        compiler_params=pltpu.CompilerParams(vmem_limit_bytes=mib(8)),
        name="join",
    )(keep, *other)


def fold_kernel(keep_ref, *refs):
    total = keep_ref[...]
    for other in refs[:-1]:
        total = total + other[...].astype(F32)
    refs[-1][...] = total


def fold(keep, arrived):
    return pl.pallas_call(
        fold_kernel,
        out_shape=jax.ShapeDtypeStruct(keep.shape, F32),
        compiler_params=pltpu.CompilerParams(vmem_limit_bytes=mib(7)),
        name="fold",
    )(keep, *arrived)


def finish_kernel(mixed_ref, total_ref, *refs):
    gains_ref, out_ref = refs[-2:]
    half = total_ref.shape[0] // 2
    for at in range(2):
        rows = slice(at * half, (at + 1) * half)
        total = total_ref[rows, :] + refs[at][...].astype(F32)
        out_ref[rows, :] = (mixed_ref[rows, :] + rms(total) * gains_ref[2:3, :]).astype(BF16)


def finish(mixed, total, other, gains):
    return pl.pallas_call(
        finish_kernel,
        out_shape=jax.ShapeDtypeStruct(mixed.shape, BF16),
        compiler_params=pltpu.CompilerParams(vmem_limit_bytes=mib(7)),
        name="finish",
    )(mixed, total, *other, gains)


def local(
    queries,
    suffix_kv,
    prefix_cache,
    q_gain,
    k_gain,
    lengths,
    group_of,
    owner_order,
    residual,
    w_out,
    attn_gain,
    ffn_in_gain,
    ffn_out_gain,
    w_gate,
    w_up,
    w_down,
):
    req_count = lax.axis_size("req")
    tok_count = lax.axis_size("tok")
    req_index = lax.axis_index("req")
    tok_index = lax.axis_index("tok")
    across = req_count // LINE
    planes = tok_count // CORES
    row_count = queries.shape[0]
    share = row_count // tok_count
    heads_here = queries.shape[1] // HD
    head_ratio = H // KVH
    kv_first = tok_index * heads_here // head_ratio
    kv_width = KVH * HD

    def head_columns(rows_in, which):
        return lax.dynamic_slice_in_dim(rows_in, which * kv_width + kv_first * HD, HD, 1)

    def move(values_in, lines, shift=0):
        pairs = [
            (source * across + col, target * across + (col + shift) % across)
            for source, target in lines
            for col in range(across)
        ]
        return lax.ppermute(values_in, "req", pairs)

    def other_core(values_in):
        return lax.ppermute(values_in, "tok", [(at, at ^ 1) for at in range(tok_count)])

    def plane_shift(values_in, shift):
        return lax.ppermute(
            values_in, "tok", [(at, (at + CORES * shift) % tok_count) for at in range(tok_count)]
        )

    own_block = jnp.concatenate([head_columns(prefix_cache, 0), head_columns(prefix_cache, 1)], axis=1)
    where = jnp.stack([req_index, tok_index, kv_first]).astype(jnp.int32)
    numbers = jnp.concatenate([where, group_of, owner_order, lengths[0]])
    gains = jnp.stack([attn_gain, ffn_in_gain, ffn_out_gain])
    numbers, gains = lax.optimization_barrier((numbers, gains))
    opening = (queries, suffix_kv, jnp.stack([q_gain, k_gain]))
    attention_on = functools.partial(attention_call, numbers, across, req_count)
    shifts = range(1, across)
    every = [(line, line) for line in range(LINE)]

    def across_all(block, table, lines=every):
        return [([move(block, lines, shift)], table, shift) for shift in shifts]

    w_far, own_block = lax.optimization_barrier((w_out, own_block))
    left = move(own_block, [(0, 1), (1, 2), (2, 3)])
    right = move(own_block, [(1, 0), (2, 1), (3, 2)])
    crossed = across_all(own_block, (0, 1, 2, 3))
    plane_weights = [w_out] + [plane_shift(w_far, shift) for shift in range(1, planes)]
    state = attention_on(opening, None, [([own_block], (0, 1, 2, 3), 0)], 0)

    first = [([left], (-1, 0, 1, 2), 0), ([right], (1, 2, 3, -1), 0)] + crossed
    left, right, _ = lax.optimization_barrier((left, right, state[1]))
    onward = move(left, [(1, 2), (2, 3)])
    back = move(right, [(2, 1), (1, 0)])
    second = [([onward], (-1, -1, 0, 1), 0), ([back], (2, 3, -1, -1), 0)]
    second += across_all(pick(numbers, across, left, right), (1, 2, 1, 2))
    second += [
        ([move(block, [(0, 1), (3, 2)])], (-1, 0, 3, -1), shift) for [block], _, shift in crossed
    ]
    state = attention_on(None, state, first, 0)

    onward, back, _ = lax.optimization_barrier((onward, back, state[1]))
    far = pick(numbers, across, onward, back)
    last = move(far, [(2, 3), (1, 0)])
    third = across_all(far, (2, 3, 0, 1))
    state = attention_on(None, state, second, 0)

    last, _ = lax.optimization_barrier((last, state[1]))
    middle = last.shape[0] // 2
    table = (3, -1, -1, 0)
    fourth = []
    for [block], _, shift in third:
        halves = [move(last[:middle], [(0, 0), (3, 3)], shift), move(block[middle:], [(2, 3), (1, 0)])]
        fourth.append((halves, table, shift))
    state = attention_on(None, state, [([last], table, 0)] + third, 0)
    attention = attention_on(None, state, fourth, planes)
    plane_weights[1:], attention = lax.optimization_barrier((plane_weights[1:], attention))

    weight_parts = [[part, other_core(part)] for part in plane_weights]
    far_weights = [part for parts in weight_parts[1:] for part in parts]
    order = list(range(planes - 1, -1, -1))
    far_heads = {}
    previous = None
    for group in order:
        sent = [attention[(group + shift) % planes] for shift in range(1, planes)]
        if previous is not None:
            sent, previous = lax.optimization_barrier((sent, previous))
        previous = [plane_shift(part, shift) for shift, part in enumerate(sent, 1)]
        far_heads[group] = previous
    own_heads = [[attention[group], other_core(attention[group])] for group in range(planes)]

    def rows_of(group):
        heads_parts = list(own_heads[group])
        for part in far_heads[group]:
            heads_parts += [part, other_core(part)]
        return feed_rows(
            numbers,
            group,
            planes,
            residual,
            heads_parts,
            weight_parts[0],
            far_weights,
            gains,
            (w_gate, w_up, w_down),
        )

    keep, *send = rows_of(order[0])
    arrived = []
    for group, later in zip(order, order[1:]):
        joined = join(keep, [other_core(part) for part in send])
        own_heads[later], joined = lax.optimization_barrier((own_heads[later], joined))
        arrived.append(plane_shift(joined, group))
        keep, *send = rows_of(later)
    *send, mixed = send
    send, arrived = lax.optimization_barrier((send, arrived))
    other = [other_core(part) for part in send]
    return finish(mixed, fold(keep, arrived), other, gains)


def solution(mesh):
    in_specs = (
        P("req", "tok"),
        P("req", None),
        P("req", None),
        P(),
        P(),
        P("req", None),
        P(),
        P(),
        P("req", None),
        P("tok", None),
        P(),
        P(),
        P(),
        P(None, "tok"),
        P(None, "tok"),
        P("tok", None),
    )
    out_specs = P(("req", "tok"), None)
    return jax.shard_map(local, mesh=mesh, in_specs=in_specs, out_specs=out_specs, check_vma=False)
```

```python
import functools

import jax
import jax.numpy as jnp
from jax import lax
from jax.experimental import pallas as pl
from jax.experimental.pallas import tpu as pltpu
from jax.sharding import PartitionSpec as P

H = 8
KVH = 4
HD = 256
GROUPS = 2
EPSILON = 1e-06
MASKED = -1e30
CORES = 2
LINE = 4
NUMBERS = 3
FEED_LIMIT = 38
BF16 = jnp.bfloat16
F32 = jnp.float32
ANY = pl.BlockSpec(memory_space=pl.ANY)
VMEM = pl.BlockSpec(memory_space=pltpu.VMEM)
SMEM = pl.BlockSpec(memory_space=pltpu.SMEM)
HBM = pl.BlockSpec(memory_space=pltpu.HBM)


def mib(count):
    return count << 20


def in_vmem(values_in):
    return pltpu.with_memory_space_constraint(values_in, pltpu.VMEM)


def in_hbm(values_in):
    return pltpu.with_memory_space_constraint(values_in, pltpu.HBM)


def rms(values_in):
    return values_in * lax.rsqrt(jnp.mean(values_in * values_in, axis=-1, keepdims=True) + EPSILON)


def attend(query_ref, state, head, rows, keys, values, visible):
    max_ref, sum_ref, acc_ref = state
    columns = slice(head * HD, (head + 1) * HD)
    scores = lax.dot_general(
        query_ref[rows, columns], keys, (((1,), (1,)), ((), ())), preferred_element_type=F32
    )
    if visible is not None:
        scores = jnp.where(visible, scores, MASKED)
        block_max = jnp.max(scores, axis=1, keepdims=True)
        weights = jnp.exp(scores - block_max)
        max_ref[head, rows, :] = jnp.broadcast_to(block_max, (scores.shape[0], 128))
        sum_ref[head, rows, :] = jnp.broadcast_to(
            jnp.sum(weights, axis=1, keepdims=True), (scores.shape[0], 128)
        )
        acc_ref[rows, columns] = jnp.dot(weights.astype(BF16), values, preferred_element_type=F32)
        return
    old_max = max_ref[head, rows, :]
    new_max = jnp.maximum(old_max, jnp.max(scores, axis=1, keepdims=True))
    scale = jnp.exp(old_max - new_max)
    weights = jnp.exp(scores - new_max[:, :1])
    max_ref[head, rows, :] = new_max
    sum_ref[head, rows, :] = sum_ref[head, rows, :] * scale + jnp.sum(weights, axis=1, keepdims=True)
    acc_ref[rows, columns] = acc_ref[rows, columns] * scale[:, :1] + jnp.dot(
        weights.astype(BF16), values, preferred_element_type=F32
    )


def block_wanted(numbers, place, across, req_count):
    source_lines, col_shift = place
    per_group = req_count // GROUPS
    req_index = numbers[0]
    line = req_index // across
    source_line = jnp.int32(-1)
    for at, source in enumerate(source_lines):
        if source >= 0:
            source_line = jnp.where(line == at, source, source_line)
    source = source_line * across + lax.rem(lax.rem(req_index, across) + across - col_shift, across)
    holder = jnp.int32(-1)
    for slot in range(req_count):
        holder = jnp.where(numbers[NUMBERS + req_count + slot] == source, slot // per_group, holder)
    return (source_line >= 0) & (holder == numbers[NUMBERS + req_index])


def attention_kernel(places, counts, across, req_count, heads, first, parts, near, *refs):
    refs = list(refs)
    take = lambda count: [refs.pop(0) for _ in range(count)]
    (numbers,) = take(1)
    if first:
        queries_ref, suffix, gains = take(3)
    else:
        query_ref, max_in, sum_in, acc_in = take(4)
    blocks = [take(count) for count in counts]
    take(near)
    if first:
        query_ref, max_ref, sum_ref, acc_ref, queries, own_keys, own_values, held, sems, own_sems = refs
    elif parts:
        out_refs = take(parts)
        max_ref, sum_ref, acc_ref, held, sems = refs
    else:
        max_ref, sum_ref, acc_ref = take(3)
        held, sems = refs
    state = (max_ref, sum_ref, acc_ref)
    wanted = [block_wanted(numbers, place, across, req_count) for place in places]

    def copies_of(at):
        extent = held.shape[1] // counts[at]
        return [
            pltpu.make_async_copy(
                block, held.at[at, pl.ds(piece * extent, extent)], sems.at[at, piece]
            )
            for piece, block in enumerate(blocks[at])
        ]

    for at in range(len(places)):

        @pl.when(wanted[at])
        def _():
            for copy in copies_of(at):
                copy.start()

    row_count = query_ref.shape[0]
    step = min(256, row_count)
    if first:
        begin = pl.multiple_of(numbers[2] * HD, HD)
        copies = [pltpu.make_async_copy(queries_ref, queries, own_sems.at[2])] + [
            pltpu.make_async_copy(
                suffix.at[:, pl.ds(pl.multiple_of(begin + which * KVH * HD, HD), HD)],
                target,
                own_sems.at[which],
            )
            for which, target in enumerate((own_keys, own_values))
        ]
        for copy in copies:
            copy.start()
        copies[0].wait()
        for head in range(heads):
            columns = slice(head * HD, (head + 1) * HD)
            normed = (rms(queries[:, columns].astype(F32)) * gains[:1, :]).astype(BF16)
            query_ref[:, columns] = normed * jnp.asarray(HD ** (-0.5), BF16)
        for copy in copies[1:]:
            copy.wait()
        own_keys[...] = (rms(own_keys[...].astype(F32)) * gains[1:, :]).astype(BF16)
        ends = []
        first_length = NUMBERS + 2 * req_count
        for at in range(first_length, numbers.shape[0] - 1):
            ends.append(numbers[at] + (ends[-1] if ends else 0))
        for begin in range(0, row_count, step):
            rows = slice(begin, begin + step)
            seen = begin + step
            row_at = lax.broadcasted_iota(jnp.int32, (step, seen), 0) + begin
            key_at = lax.broadcasted_iota(jnp.int32, (step, seen), 1)
            visible = key_at <= row_at
            for end in ends:
                visible &= (row_at < end) | (key_at >= end)
            for head in range(heads):
                attend(query_ref, state, head, rows, own_keys[:seen, :], own_values[:seen, :], visible)
    else:
        max_ref[...] = max_in[...]
        sum_ref[...] = sum_in[...]
        acc_ref[...] = acc_in[...]

    for at in range(len(places)):

        @pl.when(wanted[at])
        def _():
            for copy in copies_of(at):
                copy.wait()

            @pl.loop(0, row_count // step, unroll=2 if parts else 1)
            def _(turn):
                rows = pl.ds(pl.multiple_of(turn * step, step), step)
                for head in range(heads):
                    attend(query_ref, state, head, rows, held[at, :, :HD], held[at, :, HD:], None)


    for at in range(parts):
        extent = row_count // parts
        begin = lax.rem(numbers[1] // CORES + at, parts) * extent
        rows = pl.ds(pl.multiple_of(begin, extent), extent)
        for head in range(heads):
            columns = slice(head * HD, (head + 1) * HD)
            out_refs[at][:, columns] = (acc_ref[rows, columns] / sum_ref[head, rows, :1]).astype(BF16)


def attention_call(numbers, across, req_count, opening, state, wave, parts, near=()):
    blocks = [block for parts_of, _, _ in wave for block in parts_of]
    counts = [len(parts_of) for parts_of, _, _ in wave]
    places = [(sources, shift) for _, sources, shift in wave]
    query = opening[0] if state is None else state[0]
    row_count = query.shape[0]
    heads = query.shape[1] // HD
    shapes = [
        ((heads, row_count, 128), F32),
        ((heads, row_count, 128), F32),
        ((row_count, heads * HD), F32),
    ]
    first = state is None
    kernel = functools.partial(attention_kernel, places, counts, across, req_count, heads, first, parts, len(near))
    if first:
        queries, suffix, gains = opening
        operands = (numbers, in_hbm(queries), in_hbm(suffix), gains, *blocks)
        in_specs = [SMEM, HBM, HBM, VMEM] + [ANY] * len(blocks)
    else:
        operands = (numbers, *state, *blocks, *[in_vmem(part) for part in near])
        in_specs = [SMEM] + [VMEM] * 4 + [ANY] * len(blocks) + [VMEM] * len(near)
    scratch = [
        pltpu.VMEM((len(wave), row_count, 2 * HD), BF16),
        pltpu.SemaphoreType.DMA((len(wave), 2)),
    ]
    states = [jax.ShapeDtypeStruct(shape, dtype) for shape, dtype in shapes]
    if first:
        out_shape = [jax.ShapeDtypeStruct(query.shape, BF16)] + states
        scratch = (
            [pltpu.VMEM(query.shape, BF16)]
            + [pltpu.VMEM((row_count, HD), BF16)] * 2
            + scratch
            + [pltpu.SemaphoreType.DMA((3,))]
        )
    elif parts:
        out_shape = [jax.ShapeDtypeStruct((row_count // parts, query.shape[1]), BF16)] * parts
        scratch = [pltpu.VMEM(shape, dtype) for shape, dtype in shapes] + scratch
    else:
        out_shape = states
    result = pl.pallas_call(
        kernel,
        in_specs=in_specs,
        out_specs=[VMEM] * len(out_shape),
        out_shape=out_shape,
        scratch_shapes=scratch,
        compiler_params=pltpu.CompilerParams(vmem_limit_bytes=mib(7)),
        cost_estimate=pl.CostEstimate(
            flops=8 * row_count * row_count * heads * HD,
            bytes_accessed=mib(4),
            transcendentals=2 * row_count * row_count * heads,
        ),
        name="attend_blocks",
    )(*operands)
    return result if first or parts else [query, *result]


def pick_kernel(lines, numbers, upper_ref, lower_ref, out_ref):
    upper = numbers[0] >= lines

    @pl.when(upper)
    def _():
        out_ref[...] = upper_ref[...]

    @pl.when(jnp.logical_not(upper))
    def _():
        out_ref[...] = lower_ref[...]


def pick(numbers, across, upper, lower):
    return pl.pallas_call(
        functools.partial(pick_kernel, across * LINE // 2),
        in_specs=[SMEM, VMEM, VMEM],
        out_specs=VMEM,
        out_shape=jax.ShapeDtypeStruct(upper.shape, upper.dtype),
        compiler_params=pltpu.CompilerParams(vmem_limit_bytes=mib(4)),
        name="pick",
    )(numbers, upper, lower)


def column_step(width):
    return 512 if width % 512 == 0 else 128


def feed_kernel(pieces, group, planes, *refs):
    refs = list(refs)
    take = lambda count: [refs.pop(0) for _ in range(count)]
    (numbers,), heads_refs, (gains,) = take(1), take(pieces), take(1)
    (gate_ref,), weight_refs = take(1), take(pieces - 2)
    up_source, down_source, residual_ref, *near_sources = take(5)
    (keep_ref, *send_refs), mixed_refs = take(3), take(int(group == 0))
    spare, total_ref, normed_ref, up_ref, down_ref, sems = refs
    share, width = keep_ref.shape
    hidden = gate_ref.shape[1]
    core_at = lax.rem(numbers[1], CORES)
    first_row = lax.rem(numbers[1] // CORES + group, planes) * CORES * share
    unroll = 5
    step = 512 if hidden % 512 == 0 else 256

    def columns_of(at, extent):
        return pl.ds(at * extent if isinstance(at, int) else pl.multiple_of(at * extent, extent), extent)

    residual_copies = []
    for tile in range(CORES):
        target = pl.multiple_of(jnp.where(core_at == tile, 0, share), share)
        residual_copies.append(
            pltpu.make_async_copy(
                residual_ref.at[pl.ds(pl.multiple_of(first_row + tile * share, share), share)],
                spare.at[pl.ds(target, share), pl.ds(0, width)],
                sems.at[tile],
            )
        )
    depth = near_sources[0].shape[0]
    near_copies = [
        pltpu.make_async_copy(source, down_ref.at[pl.ds(at * depth, depth)], sems.at[CORES + at])
        for at, source in enumerate(near_sources)
    ]
    down_copies = [
        pltpu.make_async_copy(down_source.at[rows], down_ref.at[rows], sems.at[CORES + 2 + at])
        for at, rows in enumerate((pl.ds(0, 2 * depth), pl.ds(2 * depth, hidden - 2 * depth)))
    ]
    up_copies = [
        pltpu.make_async_copy(
            up_source.at[:, pl.ds(begin, step)], up_ref.at[:, pl.ds(begin, step)], sems.at[CORES + 4 + at]
        )
        for at, begin in enumerate(range(0, hidden, step))
    ]
    for copy in [*near_copies, *residual_copies, *up_copies, down_copies[1]]:
        copy.start()
    wide = column_step(width)

    @pl.loop(0, width // wide, unroll=5)
    def _(at):
        columns = columns_of(at, wide)
        total = jnp.dot(heads_refs[2][...], weight_refs[0][:, columns], preferred_element_type=F32)
        for piece in range(3, pieces):
            total += jnp.dot(
                heads_refs[piece][...], weight_refs[piece - 2][:, columns], preferred_element_type=F32
            )
        total_ref[:, columns] = total

    for copy in near_copies:
        copy.wait()

    @pl.loop(0, width // wide, unroll=5)
    def _(at):
        columns = columns_of(at, wide)
        total = total_ref[:, columns]
        for piece in range(2):
            total += jnp.dot(
                heads_refs[piece][...],
                down_ref[piece * depth : (piece + 1) * depth, columns],
                preferred_element_type=F32,
            )
        total_ref[:, columns] = total

    down_copies[0].start()
    for copy in residual_copies:
        copy.wait()
    extent = min(64, share)

    @pl.loop(0, CORES * share // extent)
    def _(at):
        rows = pl.ds(pl.multiple_of(at * extent, extent), extent)
        source = lax.rem(at * extent + core_at * share, CORES * share)
        total = total_ref[pl.ds(pl.multiple_of(source, extent), extent), :]
        mixed = spare[rows, :width].astype(F32) + rms(total) * gains[0:1, :]
        normed_ref[rows, :] = (rms(mixed) * gains[1:2, :]).astype(BF16)
        for mixed_ref in mixed_refs:

            @pl.when(at < share // extent)
            def _():
                mixed_ref[rows, :] = mixed

    for at, copy in enumerate(up_copies):
        columns = slice(at * step, (at + 1) * step)
        gate = jnp.dot(normed_ref[...], gate_ref[:, columns], preferred_element_type=F32)
        copy.wait()
        upward = jnp.dot(normed_ref[...], up_ref[:, columns], preferred_element_type=F32)
        spare[:, columns] = (jax.nn.gelu(gate, approximate=True) * upward).astype(BF16)

    for copy in down_copies:
        copy.wait()

    @pl.loop(0, width // step, unroll=unroll)
    def _(at):
        columns = columns_of(at, step)
        down = jnp.dot(spare[:, :hidden], down_ref[:, columns], preferred_element_type=F32)
        keep_ref[:, columns] = down[:share]
        for at_send, send_ref in enumerate(send_refs):
            begin = share + at_send * send_ref.shape[0]
            send_ref[:, columns] = down[begin : begin + send_ref.shape[0]].astype(BF16)


def feed_rows(
    numbers, group, planes, residual, heads_parts, near_weights, far_weights, gains, feed_weights
):
    pieces = len(heads_parts)
    rows, depth = heads_parts[0].shape
    width = residual.shape[1]
    share = rows // CORES
    hidden = feed_weights[0].shape[1]
    return pl.pallas_call(
        functools.partial(feed_kernel, pieces, group, planes),
        in_specs=[SMEM] + [VMEM] * (2 * pieces) + [HBM] * 5,
        out_specs=[VMEM] * (3 + (group == 0)),
        out_shape=[pltpu.VMEM((share, width), F32)]
        + [pltpu.VMEM((share // 2, width), BF16)] * 2
        + [pltpu.VMEM((share, width), F32)] * (group == 0),
        scratch_shapes=[
            pltpu.VMEM((rows, max(width, hidden)), BF16),
            pltpu.VMEM((rows, width), F32),
            pltpu.VMEM((rows, width), BF16),
            pltpu.VMEM((width, hidden), BF16),
            pltpu.VMEM((hidden, width), BF16),
            pltpu.SemaphoreType.DMA((CORES + 4 + hidden // 256,)),
        ],
        compiler_params=pltpu.CompilerParams(vmem_limit_bytes=mib(FEED_LIMIT)),
        cost_estimate=pl.CostEstimate(
            flops=2 * rows * width * (pieces * heads_parts[0].shape[1] + 3 * hidden),
            bytes_accessed=mib(16),
            transcendentals=rows * hidden,
        ),
        name="feed_rows",
    )(
        numbers,
        *heads_parts,
        gains,
        *[in_vmem(part) for part in (feed_weights[0], *far_weights)],
        *[in_hbm(part) for part in (*feed_weights[1:], residual, *near_weights)],
    )


def join_kernel(keep_ref, *refs):
    out_ref = refs[-1]
    half = keep_ref.shape[0] // 2
    for at in range(2):
        rows = slice(at * half, (at + 1) * half)
        out_ref[rows, :] = (keep_ref[rows, :] + refs[at][...].astype(F32)).astype(BF16)


def join(keep, other):
    return pl.pallas_call(
        join_kernel,
        out_shape=jax.ShapeDtypeStruct(keep.shape, BF16),
        compiler_params=pltpu.CompilerParams(vmem_limit_bytes=mib(8)),
        name="join",
    )(keep, *other)


def fold_kernel(keep_ref, *refs):
    total = keep_ref[...]
    for other in refs[:-1]:
        total = total + other[...].astype(F32)
    refs[-1][...] = total


def fold(keep, arrived):
    return pl.pallas_call(
        fold_kernel,
        out_shape=jax.ShapeDtypeStruct(keep.shape, F32),
        compiler_params=pltpu.CompilerParams(vmem_limit_bytes=mib(7)),
        name="fold",
    )(keep, *arrived)


def finish_kernel(mixed_ref, total_ref, *refs):
    gains_ref, out_ref = refs[-2:]
    half = total_ref.shape[0] // 2
    for at in range(2):
        rows = slice(at * half, (at + 1) * half)
        total = total_ref[rows, :] + refs[at][...].astype(F32)
        out_ref[rows, :] = (mixed_ref[rows, :] + rms(total) * gains_ref[2:3, :]).astype(BF16)


def finish(mixed, total, other, gains):
    return pl.pallas_call(
        finish_kernel,
        out_shape=jax.ShapeDtypeStruct(mixed.shape, BF16),
        compiler_params=pltpu.CompilerParams(vmem_limit_bytes=mib(7)),
        name="finish",
    )(mixed, total, *other, gains)


def local(
    queries,
    suffix_kv,
    prefix_cache,
    q_gain,
    k_gain,
    lengths,
    group_of,
    owner_order,
    residual,
    w_out,
    attn_gain,
    ffn_in_gain,
    ffn_out_gain,
    w_gate,
    w_up,
    w_down,
):
    req_count = lax.axis_size("req")
    tok_count = lax.axis_size("tok")
    req_index = lax.axis_index("req")
    tok_index = lax.axis_index("tok")
    across = req_count // LINE
    planes = tok_count // CORES
    row_count = queries.shape[0]
    share = row_count // tok_count
    heads_here = queries.shape[1] // HD
    head_ratio = H // KVH
    kv_first = tok_index * heads_here // head_ratio
    kv_width = KVH * HD

    def head_columns(rows_in, which):
        return lax.dynamic_slice_in_dim(rows_in, which * kv_width + kv_first * HD, HD, 1)

    def move(values_in, lines, shift=0):
        pairs = [
            (source * across + col, target * across + (col + shift) % across)
            for source, target in lines
            for col in range(across)
        ]
        return lax.ppermute(values_in, "req", pairs)

    def other_core(values_in):
        return lax.ppermute(values_in, "tok", [(at, at ^ 1) for at in range(tok_count)])

    def plane_shift(values_in, shift):
        return lax.ppermute(
            values_in, "tok", [(at, (at + CORES * shift) % tok_count) for at in range(tok_count)]
        )

    own_block = jnp.concatenate([head_columns(prefix_cache, 0), head_columns(prefix_cache, 1)], axis=1)
    where = jnp.stack([req_index, tok_index, kv_first]).astype(jnp.int32)
    numbers = jnp.concatenate([where, group_of, owner_order, lengths[0]])
    gains = jnp.stack([attn_gain, ffn_in_gain, ffn_out_gain])
    numbers, gains = lax.optimization_barrier((numbers, gains))
    opening = (queries, suffix_kv, jnp.stack([q_gain, k_gain]))
    attention_on = functools.partial(attention_call, numbers, across, req_count)
    shifts = range(1, across)
    every = [(line, line) for line in range(LINE)]

    def across_all(block, table, lines=every):
        return [([move(block, lines, shift)], table, shift) for shift in shifts]

    w_far, own_block = lax.optimization_barrier((w_out, own_block))
    left = move(own_block, [(0, 1), (1, 2), (2, 3)])
    right = move(own_block, [(1, 0), (2, 1), (3, 2)])
    crossed = across_all(own_block, (0, 1, 2, 3))
    plane_weights = [w_out] + [plane_shift(w_far, shift) for shift in range(1, planes)]
    state = attention_on(opening, None, [([own_block], (0, 1, 2, 3), 0)], 0)

    first = [([left], (-1, 0, 1, 2), 0), ([right], (1, 2, 3, -1), 0)] + crossed
    left, right, _ = lax.optimization_barrier((left, right, state[1]))
    onward = move(left, [(1, 2), (2, 3)])
    back = move(right, [(2, 1), (1, 0)])
    second = [([onward], (-1, -1, 0, 1), 0), ([back], (2, 3, -1, -1), 0)]
    second += across_all(pick(numbers, across, left, right), (1, 2, 1, 2))
    second += [
        ([move(block, [(0, 1), (3, 2)])], (-1, 0, 3, -1), shift) for [block], _, shift in crossed
    ]
    state = attention_on(None, state, first, 0)

    onward, back, _ = lax.optimization_barrier((onward, back, state[1]))
    far = pick(numbers, across, onward, back)
    last = move(far, [(2, 3), (1, 0)])
    third = across_all(far, (2, 3, 0, 1))
    state = attention_on(None, state, second, 0)

    last, _ = lax.optimization_barrier((last, state[1]))
    middle = last.shape[0] // 2
    table = (3, -1, -1, 0)
    fourth = []
    for [block], _, shift in third:
        halves = [move(last[:middle], [(0, 0), (3, 3)], shift), move(block[middle:], [(2, 3), (1, 0)])]
        fourth.append((halves, table, shift))
    state = attention_on(None, state, [([last], table, 0)] + third, 0)
    attention = attention_on(None, state, fourth, planes)
    plane_weights[1:], attention = lax.optimization_barrier((plane_weights[1:], attention))

    weight_parts = [[part, other_core(part)] for part in plane_weights]
    far_weights = [part for parts in weight_parts[1:] for part in parts]
    order = list(range(planes - 1, -1, -1))
    far_heads = {}
    previous = None
    for group in order:
        sent = [attention[(group + shift) % planes] for shift in range(1, planes)]
        if previous is not None:
            sent, previous = lax.optimization_barrier((sent, previous))
        previous = [plane_shift(part, shift) for shift, part in enumerate(sent, 1)]
        far_heads[group] = previous
    own_heads = [[attention[group], other_core(attention[group])] for group in range(planes)]

    def rows_of(group):
        heads_parts = list(own_heads[group])
        for part in far_heads[group]:
            heads_parts += [part, other_core(part)]
        return feed_rows(
            numbers,
            group,
            planes,
            residual,
            heads_parts,
            weight_parts[0],
            far_weights,
            gains,
            (w_gate, w_up, w_down),
        )

    keep, *send = rows_of(order[0])
    arrived = []
    for group, later in zip(order, order[1:]):
        joined = join(keep, [other_core(part) for part in send])
        own_heads[later], joined = lax.optimization_barrier((own_heads[later], joined))
        arrived.append(plane_shift(joined, group))
        keep, *send = rows_of(later)
    *send, mixed = send
    send, arrived = lax.optimization_barrier((send, arrived))
    other = [other_core(part) for part in send]
    return finish(mixed, fold(keep, arrived), other, gains)


def solution(mesh):
    in_specs = (
        P("req", "tok"),
        P("req", None),
        P("req", None),
        P(),
        P(),
        P("req", None),
        P(),
        P(),
        P("req", None),
        P("tok", None),
        P(),
        P(),
        P(),
        P(None, "tok"),
        P(None, "tok"),
        P("tok", None),
    )
    out_specs = P(("req", "tok"), None)
    return jax.shard_map(local, mesh=mesh, in_specs=in_specs, out_specs=out_specs, check_vma=False)
```
